256 devices in a mesh: section: 8 (over z), expert: 32 (over x, y, core).
Axes of the slice: x: 4, y: 4, z: 8, core: 2. Of those that a mesh axis runs over, the one named last changes fastest.
Arguments:
- residual: bfloat16 [4096, 3584], P(('section', 'expert')), may hold values from -6 to 6
- query_latent: bfloat16 [4096, 65536], P(('section', 'expert')), may hold values from -64 to 64
- query_rotary: bfloat16 [4096, 8192], P(('section', 'expert')), may hold values from -64 to 64
- cache_latent: bfloat16 [1024, 512, 512], P(('section', 'expert')), may hold values from -8 to 8
- cache_rotary: bfloat16 [1024, 64, 512], P(('section', 'expert')), may hold values from -8 to 8
- new_latent: bfloat16 [4096, 512], P(('section', 'expert')), may hold values from -6 to 6
- new_rotary: bfloat16 [64, 4096], P(None, ('section', 'expert')), may hold values from -6 to 6
- cache_len: int32 [1024], P(('section', 'expert')), may hold values from 128 to 512, as said below
- route_ids: int32 [4096, 2], P('section'), may hold values from 0 to 3, all different within a row; in each aligned block of 16 rows (0 to 15, 16 to 31, ...) at most 12 rows name the same one
- routing_weight: float32 [4096, 2], P('section'), may hold values from 0.1 to 1
- norm_gain: float32 [8, 3584], P('section'), may hold values from 0.5 to 1.5
- value_up_matrix: bfloat16 [8, 128, 512, 128], P('section', 'expert'), may hold values from -0.25 to 0.25
- out_weight: bfloat16 [8, 16384, 3584], P('section', 'expert'), may hold values from -0.1875 to 0.1875
- gate_weight: bfloat16 [8, 3584, 8192], P('section', None, 'expert'), may hold values from -0.09375 to 0.09375
- up_weight: bfloat16 [8, 3584, 8192], P('section', None, 'expert'), may hold values from -0.09375 to 0.09375
- down_weight: bfloat16 [8, 8192, 3584], P('section', 'expert'), may hold values from -0.125 to 0.125
Outputs:
- handed: bfloat16 [4096, 3584], P(('section', 'expert'))
The draws below stay inside these ranges and needn't reach their ends.
Inputs may be any that keep to these rules, and one draw needn't show every extreme that they name: `route_ids`: each row names 2 different experts; among the rows of one device no expert is named more than 12 times, and some expert reaches 12. `cache_len`: at least one sequence holds exactly 512 cached tokens.
All inputs are finite; a program needn't handle non-finite values.
Results may differ from the reference program's by a relative error of at most 0.0065.
Values may be sent and summed in bfloat16 or wider, within the bound.
A program may use at most 128 MiB of HBM per device.

```python
import math
import jax
import jax.numpy as jnp
import numpy as np
from jax import lax

D = 3584
KVL = 512
ROPE = 64
VDIM = 128
FF = 2048
EXPERTS = 4
TOPK = 2
TB = 4
CACHE = 512
HEADS = 128
ROWS_DEV = 16
CAP = 12
SEQS = 1024
TOKENS = 4096
N_SECTION = 8


def shared_keys(key):
    key_lat, key_rot = jax.random.split(key, 2)
    latent = jax.random.normal(key_lat, (SEQS, CACHE, KVL), jnp.float32)
    rotary = jax.random.normal(key_rot, (SEQS, ROPE, CACHE), jnp.float32)
    latent = latent.at[:, 2].set(latent[:, 2])
    rotary = rotary.at[:, :, 2].set(rotary[:, :, 2])
    return (latent, rotary)


def draw_cache_latent(key, part):
    latent, rotary = shared_keys(key)
    return latent.astype(jnp.bfloat16)


def draw_cache_rotary(key, part):
    latent, rotary = shared_keys(key)
    return rotary.astype(jnp.bfloat16)


def draw_query_latent(key, part):
    own_key = jax.random.fold_in(key, 11)
    values = jax.random.normal(own_key, (TOKENS, HEADS, KVL), jnp.float32)
    return values.reshape(TOKENS, HEADS * KVL).astype(jnp.bfloat16)


def draw_query_rotary(key, part):
    own_key = jax.random.fold_in(key, 12)
    values = jax.random.normal(own_key, (TOKENS, HEADS, ROPE), jnp.float32)
    return values.reshape(TOKENS, HEADS * ROPE).astype(jnp.bfloat16)


def draw_cache_len(key, part):
    own_key = jax.random.fold_in(key, 13)
    key_len, key_pick = jax.random.split(own_key)
    lengths = jax.random.randint(key_len, (SEQS,), CACHE // 4, CACHE + 1)
    chosen = jax.random.randint(key_pick, (), 0, SEQS)
    return jnp.where(jnp.arange(SEQS) == chosen, CACHE, lengths).astype(jnp.int32)


def level_of(key, extent, pieces, least, high):
    def one(dim, shards_of):
        draws = jax.random.uniform(jax.random.fold_in(jax.random.fold_in(key, 6), dim), (shards_of,), jnp.float32, least / len(pieces), high / len(pieces))
        return jnp.repeat(jnp.exp(draws), extent[dim] // shards_of).reshape((-1,) + (1,) * (len(extent) - dim - 1))

    loudness = one(*pieces[0])
    for cut in pieces[1:]:
        loudness = loudness * one(*cut)
    return loudness


def deal_out(key, own, number, rows, count, top, bound, skew):
    ranking = jax.random.permutation(key, count)
    crowded, usual = shares(count, rows * top, bound, skew, True), shares(count, rows * top, bound, skew, False)
    places = jnp.arange(count)

    def named(sizes, offset_by):
        used = int((sizes > 0).sum())
        fixed = max(1, used // 4)
        shifted = fixed + (places - fixed + offset_by * (used - fixed)) % max(1, count - fixed)
        return jnp.zeros((count,), jnp.int32).at[ranking[jnp.where(places < fixed, places, shifted)]].set(jnp.asarray(sizes, jnp.int32))

    sizes = jnp.where(number % 4 == 0, named(crowded, number // 4), named(usual, number - number // 4 - 1))
    mixed = jax.random.permutation(jax.random.fold_in(own, 3), count)
    source_of, sink = mixed[0:count // 2 * 2:2], mixed[1:count // 2 * 2:2]
    margin = jnp.minimum(sizes[source_of] - 1, bound - sizes[sink]) // 2
    margin = jnp.where((source_of == ranking[0]) | (sink == ranking[0]) | (sizes[sink] == 0), 0, jnp.maximum(margin, 0))
    shifted = jax.random.randint(jax.random.fold_in(own, 4), (count // 2,), 0, 1 << 20) % (margin + 1)
    sizes = sizes.at[source_of].add(-shifted).at[sink].add(shifted)
    items = jnp.searchsorted(jnp.cumsum(sizes), jnp.arange(rows * top), side="right").astype(jnp.int32)
    grid = items.reshape(top, rows).T
    grid = grid[jax.random.permutation(jax.random.fold_in(own, 1), rows)]
    offset_by = jax.random.randint(jax.random.fold_in(own, 2), (rows, 1), 0, top)
    return jnp.take_along_axis(grid, (jnp.arange(top)[None, :] + offset_by) % top, axis=1)


def shares(amount, total, bound, skew, full):
    loads = [(1 << 20) // math.isqrt(rank ** skew) + 1 for rank in range(1, amount + 1)]
    largest = bound if full else min(bound, max(-(-total // amount), total * loads[0] // sum(loads)))
    least = 1 if total - largest >= amount - 1 else 0
    given, spare = [largest] + [least] * (amount - 1), total - largest - least * (amount - 1)
    while spare > 0:
        movable = [i for i in range(1, amount) if given[i] < largest] or [i for i in range(1, amount) if given[i] < bound]
        pool, remaining = sum([loads[i] for i in movable]), spare
        for i in movable:
            extra = min(bound - given[i], max(1, remaining * loads[i] // pool), spare)
            given[i] = given[i] + extra
            spare = spare - extra
    return np.array(given)


def scatter_about(rng, dims, width, most, cuts=(), kind=jnp.bfloat16):
    level = level_of(rng, dims, cuts, -0.22, 0.18) if cuts else 1.0
    entries = jax.random.normal(rng, dims, jnp.float32) * width * level
    return jnp.minimum(jnp.maximum(entries, -most), most).astype(kind)


def setup_inputs(seed: int = 0) -> dict:
    key_of = jax.random.split(jax.random.key(seed), 17)
    residual = scatter_about(key_of[0], (TOKENS, D), 1.0, 6.0, ((0, 256),))
    query_latent = draw_query_latent(jax.random.fold_in(key_of[16], 71), 0)
    query_rotary = draw_query_rotary(jax.random.fold_in(key_of[16], 71), 0)
    cache_latent = draw_cache_latent(jax.random.fold_in(key_of[16], 71), 0)
    cache_rotary = draw_cache_rotary(jax.random.fold_in(key_of[16], 71), 0)
    new_latent = scatter_about(key_of[5], (TOKENS, KVL), 1.0, 6.0, ((0, 256),))
    new_rotary = scatter_about(key_of[6], (ROPE, TOKENS), 1.0, 6.0, ((1, 256),))
    cache_len = draw_cache_len(jax.random.fold_in(key_of[16], 71), 0)
    route_ids_keys = jax.random.split(jax.random.fold_in(key_of[8], 1), TOKENS // ROWS_DEV)
    route_ids_turns = jax.random.permutation(jax.random.fold_in(key_of[8], 3), TOKENS // ROWS_DEV)
    route_ids = jax.vmap(lambda own, number: deal_out(jax.random.fold_in(key_of[8], 2), own, number, ROWS_DEV, EXPERTS, TOPK, CAP, 2))(route_ids_keys, route_ids_turns).reshape((TOKENS, TOPK))
    routing_weight = jnp.clip(jnp.exp(math.log(1.0) - 2.3025851 * jax.random.uniform(key_of[9], (TOKENS, TOPK), jnp.float32) ** level_of(key_of[9], (TOKENS, TOPK), ((0, 8),), -0.2, 0.2)), 0.1, 1.0)
    norm_gain = jnp.clip(1.0 + 0.1 * jax.random.normal(key_of[10], (N_SECTION, D), jnp.float32), 0.5, 1.5)
    value_up_matrix = scatter_about(key_of[11], (N_SECTION, HEADS, KVL, VDIM), KVL ** -0.5, 0.25, ((0, 8), (1, 32)))
    out_weight = scatter_about(key_of[12], (N_SECTION, HEADS * VDIM, D), (HEADS * VDIM // 16) ** -0.5, 0.1875, ((0, 8), (1, 32)))
    gate_weight = scatter_about(key_of[13], (N_SECTION, D, EXPERTS * FF), D ** -0.5, 0.09375, ((0, 8), (2, 32)))
    up_weight = scatter_about(key_of[14], (N_SECTION, D, EXPERTS * FF), D ** -0.5, 0.09375, ((0, 8), (2, 32)))
    down_weight = scatter_about(key_of[15], (N_SECTION, EXPERTS * FF, D), FF ** -0.5, 0.125, ((0, 8), (1, 32)))
    return dict(residual=residual, query_latent=query_latent, query_rotary=query_rotary, cache_latent=cache_latent, cache_rotary=cache_rotary, new_latent=new_latent, new_rotary=new_rotary, cache_len=cache_len, route_ids=route_ids, routing_weight=routing_weight, norm_gain=norm_gain, value_up_matrix=value_up_matrix, out_weight=out_weight, gate_weight=gate_weight, up_weight=up_weight, down_weight=down_weight)


def attend_latent_heads(query_latent, query_rotary, cache_latent, cache_rotary, new_latent, new_rotary, length):
    block_len = query_latent.shape[0]
    head_count = query_latent.shape[1]
    keys_all = jnp.concatenate([cache_latent, new_latent], axis=0)
    rotary_all = jnp.concatenate([cache_rotary, new_rotary], axis=1)
    flat_latent = query_latent.reshape(block_len * head_count, query_latent.shape[2])
    flat_rotary = query_rotary.reshape(block_len * head_count, query_rotary.shape[2])
    scores = jnp.dot(flat_latent, keys_all.T, preferred_element_type=jnp.float32)
    scores = scores + jnp.dot(flat_rotary, rotary_all, preferred_element_type=jnp.float32)
    scores = scores * (VDIM + ROPE) ** (-0.5)
    cached = cache_latent.shape[0]
    position = jnp.arange(cached + block_len, dtype=jnp.int32)[None, :]
    token_pos = (jnp.arange(block_len * head_count, dtype=jnp.int32) // head_count)[:, None]
    visible = jnp.where(position < cached, position < length, position - cached <= token_pos)
    scores = jnp.where(visible, scores, -1e+30)
    largest = lax.optimization_barrier(jnp.max(scores, axis=1, keepdims=True))
    exponents = jnp.exp(scores - largest)
    probability = (exponents / lax.optimization_barrier(jnp.sum(exponents, axis=1, keepdims=True))).astype(jnp.bfloat16)
    context_vectors = jnp.dot(probability, keys_all, preferred_element_type=jnp.float32).astype(jnp.bfloat16)
    return context_vectors.reshape(block_len, head_count, keys_all.shape[1])

def attend_packed(packed):
    return attend_latent_heads(*packed)

def section_layer(packed):
    residual, query_latent, query_rotary, cache_latent, cache_rotary, new_latent, new_rotary, cache_len, route_ids, routing_weight, norm_gain, value_up_matrix, out_weight, gate_weight, up_weight, down_weight = packed
    row_count = residual.shape[0]
    sequences = cache_len.shape[0]
    head_count = value_up_matrix.shape[0]
    lat_query = query_latent.reshape(sequences, TB, head_count, KVL)
    rot_query = query_rotary.reshape(sequences, TB, head_count, ROPE)
    lat_new = new_latent.reshape(sequences, TB, KVL)
    rot_new = new_rotary.reshape(ROPE, sequences, TB).transpose(1, 0, 2)
    context_vectors = lax.map(attend_packed, (lat_query, rot_query, cache_latent, cache_rotary, lat_new, rot_new, cache_len))
    context_vectors = context_vectors.reshape(row_count, head_count, KVL)
    head_output = jnp.einsum('cio,iop->cip', context_vectors.astype(jnp.float32), value_up_matrix.astype(jnp.float32)).astype(jnp.bfloat16)
    attention = jnp.dot(head_output.reshape(row_count, head_count * VDIM), out_weight, preferred_element_type=jnp.float32)
    hidden = residual.astype(jnp.float32) + attention
    normed = (hidden * lax.rsqrt(lax.optimization_barrier(jnp.mean(hidden * hidden, axis=1, keepdims=True)) + 1e-06) * norm_gain[None, :]).astype(jnp.bfloat16)

    def add_expert(running, expert_id):
        gate_cols = lax.dynamic_slice_in_dim(gate_weight, expert_id * FF, FF, 1)
        up_cols = lax.dynamic_slice_in_dim(up_weight, expert_id * FF, FF, 1)
        down_rows = lax.dynamic_slice_in_dim(down_weight, expert_id * FF, FF, 0)
        gate_val = jnp.dot(normed, gate_cols, preferred_element_type=jnp.float32)
        up_val = jnp.dot(normed, up_cols, preferred_element_type=jnp.float32)
        activation_value = (jax.nn.silu(gate_val) * up_val).astype(jnp.bfloat16)
        expert_out = jnp.dot(activation_value, down_rows, preferred_element_type=jnp.float32)
        chosen = lax.optimization_barrier(jnp.sum(routing_weight * (route_ids == expert_id).astype(jnp.float32), axis=1))
        return (running + chosen[:, None] * expert_out, None)
    expert_mix, unused = lax.scan(add_expert, jnp.zeros((row_count, D), jnp.float32), jnp.arange(EXPERTS, dtype=jnp.int32))
    return (hidden + expert_mix).astype(jnp.bfloat16)

def reference(residual, query_latent, query_rotary, cache_latent, cache_rotary, new_latent, new_rotary, cache_len, route_ids, routing_weight, norm_gain, value_up_matrix, out_weight, gate_weight, up_weight, down_weight):
    sections = norm_gain.shape[0]
    per_section = residual.shape[0] // sections
    seq_section = cache_len.shape[0] // sections

    def split_rows(array):
        return array.reshape((sections, per_section) + array.shape[1:])

    def split_seqs(array):
        return array.reshape((sections, seq_section) + array.shape[1:])
    rot_new = new_rotary.reshape(ROPE, sections, per_section).transpose(1, 0, 2)
    layer_out = lax.map(section_layer, (split_rows(residual), split_rows(query_latent), split_rows(query_rotary), split_seqs(cache_latent), split_seqs(cache_rotary), split_rows(new_latent), rot_new, split_seqs(cache_len), split_rows(route_ids), split_rows(routing_weight), norm_gain, value_up_matrix, out_weight, gate_weight, up_weight, down_weight))
    layer_out = layer_out.reshape(sections * per_section, D)
    return jnp.roll(layer_out, per_section, axis=0)
```

```python
import jax
import jax.numpy as jnp
from jax import lax
from jax.experimental import pallas as pl
from jax.experimental.pallas import tpu as pltpu
from jax.sharding import PartitionSpec as P

D = 3584
KVL = 512
ROPE = 64
VDIM = 128
HEADS = 128
TB = 4
SEQ = 4
ROWS = 16
CACHE = 512
FF_DEV = 256
SIDE = 4
GROUP = 32
CHUNKS = 4
WIDE = D // CHUNKS
HALF = GROUP * ROWS // 2

BF16 = jnp.bfloat16
F32 = jnp.float32


def dot(a, b):
    return lax.dot_general(a, b, (((1,), (0,)), ((), ())), preferred_element_type=F32)


def dot_t(a, b):
    return lax.dot_general(a, b, (((1,), (1,)), ((), ())), preferred_element_type=F32)


def iota(shape, dim):
    return lax.broadcasted_iota(jnp.int32, shape, dim)


def layer_kernel(
    sections,
    residual_hbm,
    query_hbm,
    query_rot_hbm,
    latent_hbm,
    rotary_hbm,
    new_latent,
    new_rotary,
    cache_len,
    route_ids,
    routing_weight,
    norm_gain,
    value_up_hbm,
    out_weight_hbm,
    gate_hbm,
    up_hbm,
    down_hbm,
    out_hbm,
    residual,
    query,
    query_rot,
    latent,
    rotary,
    value_up,
    out_weight,
    gate_up,
    down,
    query_seq,
    rot_seq,
    keys_new,
    rot_new,
    context,
    arrived,
    diagonal,
    heads,
    chosen_all,
    chosen,
    cross_out,
    cross_in,
    first_out,
    first_in,
    second_out,
    second_in,
    hidden,
    gathered,
    hidden_units,
    activation,
    handed,
    load_sem,
    seq_sem,
    context_send,
    context_recv,
    sum_send,
    sum_recv,
    gather_send,
    gather_recv,
    hand_send,
    hand_recv,
):
    section = lax.axis_index("section")
    me = lax.axis_index("expert")
    core = me % 2
    chip = me // 2
    x = chip // SIDE
    y = chip % SIDE
    sibling = chip * 2 + 1 - core

    def device(chip_x, chip_y):
        return (chip_x * SIDE + chip_y) * 2 + core

    barrier = pltpu.get_barrier_semaphore()

    @pl.loop(1, GROUP)
    def _(offset):
        pl.semaphore_signal(barrier, inc=1, device_id={"expert": (me + offset) % GROUP})

    if sections > 1:
        pl.semaphore_signal(barrier, inc=1, device_id={"section": (section + 1) % sections})
        pl.semaphore_signal(
            barrier, inc=1, device_id={"section": (section + sections - 1) % sections}
        )

    loads = []

    def load(source, target, sem):
        copy = pltpu.make_async_copy(source, target, sem)
        copy.start()
        return copy

    load_query = load(query_hbm, query, load_sem.at[0])
    load_rot = load(query_rot_hbm, query_rot, load_sem.at[1])
    for b in range(SEQ):
        load(latent_hbm.at[b], latent.at[b], seq_sem.at[0, b])
        load(rotary_hbm.at[b], rotary.at[b], seq_sem.at[1, b])
    load_up = [
        load(value_up_hbm.at[0, j], value_up.at[:, pl.ds(j * VDIM, VDIM)], load_sem.at[2 + j])
        for j in range(4)
    ]
    load_out = load(out_weight_hbm.at[0], out_weight, load_sem.at[6])
    load_res = load(residual_hbm, residual, load_sem.at[7])
    load_gate = load(gate_hbm.at[0], gate_up.at[:, pl.ds(0, FF_DEV)], load_sem.at[8])
    load_upw = load(up_hbm.at[0], gate_up.at[:, pl.ds(FF_DEV, FF_DEV)], load_sem.at[9])
    load_down = load(down_hbm.at[0], down, load_sem.at[10])

    keys_new[...] = jnp.zeros_like(keys_new)
    keys_new[pl.ds(0, ROWS), :] = new_latent[...]
    twice = (iota((ROPE, 128), 1) % ROPE == iota((ROPE, 128), 0)).astype(BF16)
    rot_new[...] = jnp.zeros_like(rot_new)
    rot_new[pl.ds(0, ROWS), :] = dot(new_rotary[...], twice).astype(BF16)

    expert = x
    weight_row = jnp.sum(
        jnp.where(route_ids[...] == expert, routing_weight[...], 0.0), axis=0, keepdims=True
    )
    chosen_all[...] = jnp.broadcast_to(weight_row, (128, GROUP * ROWS)).T
    for side in range(2):
        for place in range(GROUP // 2):
            source = (place * 2 + (core + side) % 2) * ROWS
            chosen[pl.ds((side * 16 + place) * ROWS, ROWS), :] = chosen_all[
                pl.ds(pl.multiple_of(source, ROWS), ROWS), :
            ]

    row_to = iota((256, 256), 0)
    row_from = iota((256, 256), 1)
    permute = (
        row_from == (row_to % 64) // TB * ROWS + row_to // 64 * TB + row_to % TB
    ).astype(BF16)
    low = iota((ROWS, 128), 1) < ROPE
    load_query.wait()
    load_rot.wait()
    for g in range(8):
        pieces, rot_pieces = [], []
        for h in range(g * 16, g * 16 + 16):
            pieces.append(query[:, pl.ds(h * KVL, KVL)])
            pair = query_rot[:, pl.ds(h // 2 * 128, 128)]
            keep = low if h % 2 == 0 else jnp.logical_not(low)
            rot_pieces.append(jnp.where(keep, pair, jnp.zeros_like(pair)))
        moved = dot(permute, jnp.concatenate(pieces, axis=0)).astype(BF16)
        moved_rot = dot(permute, jnp.concatenate(rot_pieces, axis=0)).astype(BF16)
        for b in range(SEQ):
            query_seq[b, pl.ds(g * 64, 64), :] = moved[b * 64 : b * 64 + 64]
            rot_seq[b, pl.ds(g * 64, 64), :] = moved_rot[b * 64 : b * 64 + 64]

    pl.semaphore_wait(barrier, GROUP - 1 + (2 if sections > 1 else 0))

    scale = (VDIM + ROPE) ** -0.5
    tile = 256

    @pl.loop(0, SEQ)
    def _(b):
        pltpu.make_async_copy(latent_hbm.at[b], latent.at[b], seq_sem.at[0, b]).wait()
        pltpu.make_async_copy(rotary_hbm.at[b], rotary.at[b], seq_sem.at[1, b]).wait()
        keys = latent[b]
        rot_keys = jnp.concatenate([rotary[b], rotary[b]], axis=0)
        length = cache_len[b]
        for part in range(TB * HEADS // tile):
            rows = pl.ds(part * tile, tile)
            q = query_seq[b, rows, :]
            q_rot = rot_seq[b, rows, :]
            s = (dot_t(q, keys) + dot(q_rot, rot_keys)) * scale
            s_new = (dot_t(q, keys_new[...]) + dot_t(q_rot, rot_new[...])) * scale
            s = jnp.where(iota((tile, CACHE), 1) < length, s, -1e30)
            col = iota((tile, 128), 1)
            seen = jnp.logical_and(col // TB == b, col % TB <= iota((tile, 128), 0) % TB)
            s_new = jnp.where(seen, s_new, -1e30)
            top = jnp.maximum(
                jnp.max(s, axis=1, keepdims=True), jnp.max(s_new, axis=1, keepdims=True)
            )
            e = jnp.exp(s - top)
            e_new = jnp.exp(s_new - top)
            total = jnp.sum(e, axis=1, keepdims=True) + jnp.sum(e_new, axis=1, keepdims=True)
            mixed = dot(e.astype(BF16), keys) + dot(e_new.astype(BF16), keys_new[...])
            context[b, rows, :] = (mixed / total).astype(BF16)

        own = pl.ds(pl.multiple_of(me * ROWS, ROWS), ROWS)
        arrived[b, pl.ds(pl.multiple_of(chip * ROWS, ROWS), ROWS), :] = context[b, own, :]

        @pl.loop(1, GROUP)
        def _(offset):
            to = (me + offset) % GROUP
            place = (to + me) % 2 * 16 + chip
            pltpu.make_async_remote_copy(
                src_ref=context.at[b, pl.ds(pl.multiple_of(to * ROWS, ROWS), ROWS), :],
                dst_ref=arrived.at[b, pl.ds(pl.multiple_of(place * ROWS, ROWS), ROWS), :],
                send_sem=context_send.at[b],
                recv_sem=context_recv.at[b],
                device_id={"expert": to},
            ).start()

    for copy in load_up:
        copy.wait()
    sent = pl.ds(0, (GROUP - 1) * ROWS)
    same_head = iota((512, 512), 0) % ROWS // TB == iota((512, 512), 1) // VDIM
    for b in range(SEQ):
        pltpu.make_async_copy(arrived.at[b, sent], arrived.at[b, sent], context_recv.at[b]).wait()
        product = dot(arrived[b], value_up[...])
        diagonal[b] = jnp.where(same_head, product, 0.0).astype(BF16)
    out_row = iota((64, 256), 0)
    in_row = iota((64, 256), 1)
    join = (
        (out_row // ROWS == in_row % 64 // ROWS)
        & (out_row % ROWS // TB == in_row // 64)
        & (out_row % TB == in_row % TB)
    ).astype(BF16)
    for g in range(8):
        group = jnp.concatenate([diagonal[b, pl.ds(g * 64, 64), :] for b in range(SEQ)], axis=0)
        heads[pl.ds(g * 64, 64), :] = dot(join, group).astype(BF16)

    started = []

    def send(source, target, send_sem, recv_sem, to):
        copy = pltpu.make_async_remote_copy(
            src_ref=source, dst_ref=target, send_sem=send_sem, recv_sem=recv_sem, device_id=to
        )
        copy.start()
        started.append(copy)
        return copy

    def reduce_rows(which, partial, finish):
        crossing, first, second = [], [], []

        def cross(k):
            cross_out[which, k] = partial(k, 1).astype(BF16)
            crossing.append(
                send(
                    cross_out.at[which, k],
                    cross_in.at[which, k],
                    sum_send.at[which, k, 0],
                    sum_recv.at[which, k, 0],
                    {"expert": sibling},
                )
            )

        cross(0)
        cross(1)
        for k in range(CHUNKS):
            mine = partial(k, 0)
            crossing[k].wait_recv()
            first_out[which, k] = (
                (mine + cross_in[which, k].astype(F32))
                .astype(BF16)
                .reshape(SIDE, SIDE, ROWS, WIDE)
            )
            copies = []
            for offset in range(1, SIDE):
                if k % 2 == 0:
                    to = (x + offset) % SIDE
                    source = first_out.at[which, k, to]
                    where = device(to, y)
                else:
                    to = (y + offset) % SIDE
                    source = first_out.at[which, k, :, to]
                    where = device(x, to)
                copies.append(
                    send(
                        source,
                        first_in.at[which, k, offset - 1],
                        sum_send.at[which, k, offset],
                        sum_recv.at[which, k, offset],
                        {"expert": where},
                    )
                )
            first.append(copies)
            if k + 2 < CHUNKS:
                cross(k + 2)
        for k in range(CHUNKS):
            for copy in first[k]:
                copy.wait_recv()
            if k % 2 == 0:
                rows = first_out[which, k, x].astype(F32)
            else:
                rows = first_out[which, k, :, y].astype(F32)
            for slot in range(SIDE - 1):
                rows = rows + first_in[which, k, slot].astype(F32)
            second_out[which, k] = rows.astype(BF16)
            copies = []
            for offset in range(1, SIDE):
                if k % 2 == 0:
                    to = (y + offset) % SIDE
                    where = device(x, to)
                else:
                    to = (x + offset) % SIDE
                    where = device(to, y)
                copies.append(
                    send(
                        second_out.at[which, k, to],
                        second_in.at[which, k, offset - 1],
                        sum_send.at[which, k, 3 + offset],
                        sum_recv.at[which, k, 3 + offset],
                        {"expert": where},
                    )
                )
            second.append(copies)
        for k in range(CHUNKS):
            for copy in second[k]:
                copy.wait_recv()
            rows = second_out[which, k, y if k % 2 == 0 else x].astype(F32)
            for slot in range(SIDE - 1):
                rows = rows + second_in[which, k, slot].astype(F32)
            finish(k, rows)

    load_out.wait()
    load_res.wait()

    def projected(k, side):
        return dot(heads[pl.ds(side * HALF, HALF), :], out_weight[:, pl.ds(k * WIDE, WIDE)])

    squares = []

    def add_residual(k, rows):
        rows = rows + residual[:, pl.ds(k * WIDE, WIDE)].astype(F32)
        hidden[k] = rows
        squares.append(jnp.sum(rows * rows, axis=1, keepdims=True))

    reduce_rows(0, projected, add_residual)
    mean = sum(squares[1:], squares[0]) * (1.0 / D)
    factor = lax.rsqrt(mean + 1e-06)

    def block(k, side, across):
        return gathered.at[k, side, across] if k % 2 == 0 else gathered.at[k, side, :, across]

    near, far, handed_over = [], [], []
    for k in range(CHUNKS):
        gathered[k, 0, x, y] = (
            hidden[k] * factor * norm_gain[:, pl.ds(k * WIDE, WIDE)]
        ).astype(BF16)
        copies = []
        for offset in range(1, SIDE):
            where = device(x, (y + offset) % SIDE) if k % 2 == 0 else device((x + offset) % SIDE, y)
            copies.append(
                send(
                    gathered.at[k, 0, x, y],
                    gathered.at[k, 0, x, y],
                    gather_send.at[k, offset - 1],
                    gather_recv.at[k, offset - 1],
                    {"expert": where},
                )
            )
        near.append(copies)

    def to_sibling(k, across, slot):
        return send(
            block(k, 0, across),
            block(k, 1, across),
            gather_send.at[k, 6 + slot],
            gather_recv.at[k, 6 + slot],
            {"expert": sibling},
        )

    for k in range(CHUNKS):
        for copy in near[k]:
            copy.wait_recv()
        here = x if k % 2 == 0 else y
        copies = []
        for offset in range(1, SIDE):
            where = device((x + offset) % SIDE, y) if k % 2 == 0 else device(x, (y + offset) % SIDE)
            copies.append(
                send(
                    block(k, 0, here),
                    block(k, 0, here),
                    gather_send.at[k, 2 + offset],
                    gather_recv.at[k, 2 + offset],
                    {"expert": where},
                )
            )
        far.append(copies)
        handed_over.append([to_sibling(k, here, 0)])

    load_gate.wait()
    load_upw.wait()

    def add_units(k, side):
        rows = gathered[k, side].reshape(HALF, WIDE)
        product = dot(rows, gate_up[pl.ds(k * WIDE, WIDE), :])
        if k == 0:
            hidden_units[side] = product
        else:
            hidden_units[side] = hidden_units[side] + product

    for k in range(CHUNKS):
        here = x if k % 2 == 0 else y
        for offset in range(1, SIDE):
            far[k][offset - 1].wait_recv()
            handed_over[k].append(to_sibling(k, (here + SIDE - offset) % SIDE, offset))
        add_units(k, 0)
    for k in range(CHUNKS):
        for copy in handed_over[k]:
            copy.wait_recv()
        add_units(k, 1)

    def activate(side):
        gate_value = hidden_units[side, :, pl.ds(0, FF_DEV)]
        up_value = hidden_units[side, :, pl.ds(FF_DEV, FF_DEV)]
        activation[side] = (gate_value * jax.nn.sigmoid(gate_value) * up_value).astype(BF16)

    activate(1)
    activate(0)
    load_down.wait()

    def expert_share(k, side):
        product = dot(activation[side], down[:, pl.ds(k * WIDE, WIDE)])
        weight = chosen[pl.ds(side * HALF, HALF), :]
        return product * jnp.concatenate([weight] * (WIDE // 128), axis=1)

    handing = []

    def hand_over(k, rows):
        handed[k] = (hidden[k] + rows).astype(BF16)
        target = out_hbm.at[:, pl.ds(k * WIDE, WIDE)]
        if sections > 1:
            handing.append(
                send(
                    handed.at[k],
                    target,
                    hand_send.at[k],
                    hand_recv.at[k],
                    {"section": (section + 1) % sections},
                )
            )
        else:
            load(handed.at[k], target, hand_recv.at[k]).wait()

    reduce_rows(1, expert_share, hand_over)
    for copy in handing:
        copy.wait_recv()
    for copy in started:
        copy.wait_send()
    for b in range(SEQ):
        pltpu.make_async_copy(context.at[b, sent], context.at[b, sent], context_send.at[b]).wait()


def local(
    residual,
    query_latent,
    query_rotary,
    cache_latent,
    cache_rotary,
    new_latent,
    new_rotary,
    cache_len,
    route_ids,
    routing_weight,
    norm_gain,
    value_up_matrix,
    out_weight,
    gate_weight,
    up_weight,
    down_weight,
):
    sections = lax.axis_size("section")
    far = pl.BlockSpec(memory_space=pl.ANY)
    near = pl.BlockSpec(memory_space=pltpu.VMEM)
    scalar = pl.BlockSpec(memory_space=pltpu.SMEM)
    dma = pltpu.SemaphoreType.DMA
    scratch = [
        pltpu.VMEM((ROWS, D), BF16),
        pltpu.VMEM((ROWS, HEADS * KVL), BF16),
        pltpu.VMEM((ROWS, HEADS * ROPE), BF16),
        pltpu.VMEM((SEQ, CACHE, KVL), BF16),
        pltpu.VMEM((SEQ, ROPE, CACHE), BF16),
        pltpu.VMEM((KVL, 4 * VDIM), BF16),
        pltpu.VMEM((4 * VDIM, D), BF16),
        pltpu.VMEM((D, 2 * FF_DEV), BF16),
        pltpu.VMEM((FF_DEV, D), BF16),
        pltpu.VMEM((SEQ, TB * HEADS, KVL), BF16),
        pltpu.VMEM((SEQ, TB * HEADS, 128), BF16),
        pltpu.VMEM((128, KVL), BF16),
        pltpu.VMEM((128, 128), BF16),
        pltpu.VMEM((SEQ, TB * HEADS, KVL), BF16),
        pltpu.VMEM((SEQ, TB * HEADS, KVL), BF16),
        pltpu.VMEM((SEQ, TB * HEADS, KVL), BF16),
        pltpu.VMEM((GROUP * ROWS, 4 * VDIM), BF16),
        pltpu.VMEM((GROUP * ROWS, 128), F32),
        pltpu.VMEM((GROUP * ROWS, 128), F32),
        pltpu.VMEM((2, CHUNKS, HALF, WIDE), BF16),
        pltpu.VMEM((2, CHUNKS, HALF, WIDE), BF16),
        pltpu.VMEM((2, CHUNKS, SIDE, SIDE, ROWS, WIDE), BF16),
        pltpu.VMEM((2, CHUNKS, SIDE - 1, SIDE, ROWS, WIDE), BF16),
        pltpu.VMEM((2, CHUNKS, SIDE, ROWS, WIDE), BF16),
        pltpu.VMEM((2, CHUNKS, SIDE - 1, ROWS, WIDE), BF16),
        pltpu.VMEM((CHUNKS, ROWS, WIDE), F32),
        pltpu.VMEM((CHUNKS, 2, SIDE, SIDE, ROWS, WIDE), BF16),
        pltpu.VMEM((2, HALF, 2 * FF_DEV), F32),
        pltpu.VMEM((2, HALF, FF_DEV), BF16),
        pltpu.VMEM((CHUNKS, ROWS, WIDE), BF16),
        dma((11,)),
        dma((2, SEQ)),
        dma((SEQ,)),
        dma((SEQ,)),
        dma((2, CHUNKS, 7)),
        dma((2, CHUNKS, 7)),
        dma((CHUNKS, 10)),
        dma((CHUNKS, 10)),
        dma((CHUNKS,)),
        dma((CHUNKS,)),
    ]

    def kernel(*refs):
        layer_kernel(sections, *refs)

    return pl.pallas_call(
        kernel,
        out_shape=jax.ShapeDtypeStruct((ROWS, D), BF16),
        in_specs=[far] * 5 + [near, near, scalar, near, near, near] + [far] * 5,
        out_specs=far,
        scratch_shapes=scratch,
        compiler_params=pltpu.CompilerParams(
            collective_id=0, has_side_effects=True, vmem_limit_bytes=60 * 1024 * 1024
        ),
        name="layer",
    )(
        residual,
        query_latent,
        query_rotary,
        cache_latent,
        cache_rotary,
        new_latent,
        new_rotary.T,
        cache_len,
        route_ids.T,
        routing_weight.T,
        norm_gain,
        value_up_matrix,
        out_weight,
        gate_weight,
        up_weight,
        down_weight,
    )


def solution(mesh):
    rows = P(("section", "expert"), None)
    placed = (
        rows,
        rows,
        rows,
        P(("section", "expert"), None, None),
        P(("section", "expert"), None, None),
        rows,
        P(None, ("section", "expert")),
        P(("section", "expert")),
        P("section", None),
        P("section", None),
        P("section", None),
        P("section", "expert", None, None),
        P("section", "expert", None),
        P("section", None, "expert"),
        P("section", None, "expert"),
        P("section", "expert", None),
    )
    return jax.shard_map(local, mesh=mesh, in_specs=placed, out_specs=rows, check_vma=False)
```

```python
import jax
import jax.numpy as jnp
from jax import lax
from jax.experimental import pallas as pl
from jax.experimental.pallas import tpu as pltpu
from jax.sharding import PartitionSpec as P

D = 3584
KVL = 512
ROPE = 64
VDIM = 128
HEADS = 128
TB = 4
SEQ = 4
ROWS = 16
CACHE = 512
FF_DEV = 256
SIDE = 4
GROUP = 32
BATCHES = 2
PARTS = 2
CHUNKS = BATCHES * PARTS
WIDE = D // 2 // PARTS
HALF = GROUP * ROWS // 2
SHORT = ROWS // BATCHES

BF16 = jnp.bfloat16
F32 = jnp.float32


def dot(a, b):
    return lax.dot_general(a, b, (((1,), (0,)), ((), ())), preferred_element_type=F32)


def dot_t(a, b):
    return lax.dot_general(a, b, (((1,), (1,)), ((), ())), preferred_element_type=F32)


def iota(shape, dim):
    return lax.broadcasted_iota(jnp.int32, shape, dim)


def layer_kernel(
    sections,
    residual_hbm,
    query_hbm,
    query_rot_hbm,
    latent_hbm,
    rotary_hbm,
    new_latent,
    new_rotary,
    cache_len,
    route_ids,
    routing_weight,
    norm_gain,
    value_up_hbm,
    out_weight_hbm,
    gate_hbm,
    up_hbm,
    down_hbm,
    out_hbm,
    residual,
    query,
    query_rot,
    latent,
    rotary,
    value_up,
    out_weight,
    gate_up,
    down,
    query_seq,
    rot_seq,
    keys_new,
    rot_new,
    context,
    arrived,
    diagonal,
    heads,
    chosen_all,
    chosen,
    cross_out,
    cross_in,
    first_out,
    first_in,
    second_out,
    second_in,
    hidden,
    gathered,
    hidden_units,
    activation,
    mixed_rows,
    handed,
    load_sem,
    context_send,
    context_recv,
    sum_send,
    sum_recv,
    gather_send,
    near_recv,
    far_recv,
    over_recv,
    hand_sem,
):
    section = lax.axis_index("section")
    me = lax.axis_index("expert")
    core = me % 2
    chip = me // 2
    x = chip // SIDE
    y = chip % SIDE
    sibling = chip * 2 + 1 - core

    def device(chip_x, chip_y):
        return (chip_x * SIDE + chip_y) * 2 + core

    barrier = pltpu.get_barrier_semaphore()

    @pl.loop(1, GROUP)
    def _(offset):
        pl.semaphore_signal(barrier, inc=1, device_id={"expert": (me + offset) % GROUP})

    if sections > 1:
        pl.semaphore_signal(barrier, inc=1, device_id={"section": (section + 1) % sections})
        pl.semaphore_signal(
            barrier, inc=1, device_id={"section": (section + sections - 1) % sections}
        )

    def load(source, target, sem):
        copy = pltpu.make_async_copy(source, target, sem)
        copy.start()
        return copy

    load_query = load(query_hbm, query, load_sem.at[0])
    load_rot = load(query_rot_hbm, query_rot, load_sem.at[1])
    load_latent = load(latent_hbm, latent, load_sem.at[2])
    load_rotary = load(rotary_hbm, rotary, load_sem.at[3])
    for j in range(4):
        load(value_up_hbm.at[0, j], value_up.at[:, pl.ds(j * VDIM, VDIM)], load_sem.at[4])
    load_out = load(out_weight_hbm.at[0], out_weight, load_sem.at[5])
    load_res = load(residual_hbm, residual, load_sem.at[6])
    load(gate_hbm.at[0], gate_up.at[:, pl.ds(0, FF_DEV)], load_sem.at[7])
    load(up_hbm.at[0], gate_up.at[:, pl.ds(FF_DEV, FF_DEV)], load_sem.at[7])
    load_down = load(down_hbm.at[0], down, load_sem.at[8])

    def settle(like, sem):
        pltpu.make_async_copy(like, like, sem).wait()

    keys_new[...] = jnp.zeros_like(keys_new)
    keys_new[pl.ds(0, ROWS), :] = new_latent[...]
    twice = (iota((ROPE, 128), 1) % ROPE == iota((ROPE, 128), 0)).astype(BF16)
    rot_new[...] = jnp.zeros_like(rot_new)
    rot_new[pl.ds(0, ROWS), :] = dot(new_rotary[...], twice).astype(BF16)

    expert = x
    weight_row = jnp.sum(
        jnp.where(route_ids[...] == expert, routing_weight[...], 0.0), axis=0, keepdims=True
    )
    chosen_all[...] = jnp.broadcast_to(weight_row, (128, GROUP * ROWS)).T
    for side in range(2):
        for place in range(GROUP // 2):
            source = (place * 2 + (core + side) % 2) * ROWS
            chosen[pl.ds((side * 16 + place) * ROWS, ROWS), :] = chosen_all[
                pl.ds(pl.multiple_of(source, ROWS), ROWS), :
            ]

    row_to = iota((256, 256), 0)
    row_from = iota((256, 256), 1)
    permute = (
        row_from == (row_to % 64) // TB * ROWS + row_to // 64 * TB + row_to % TB
    ).astype(BF16)
    low = iota((ROWS, 128), 1) < ROPE
    load_query.wait()
    load_rot.wait()
    for g in range(8):
        pieces, rot_pieces = [], []
        for h in range(g * 16, g * 16 + 16):
            pieces.append(query[:, pl.ds(h * KVL, KVL)])
            pair = query_rot[:, pl.ds(h // 2 * 128, 128)]
            keep = low if h % 2 == 0 else jnp.logical_not(low)
            rot_pieces.append(jnp.where(keep, pair, jnp.zeros_like(pair)))
        moved = dot(permute, jnp.concatenate(pieces, axis=0)).astype(BF16)
        moved_rot = dot(permute, jnp.concatenate(rot_pieces, axis=0)).astype(BF16)
        for b in range(SEQ):
            query_seq[b, pl.ds(g * 64, 64), :] = moved[b * 64 : b * 64 + 64]
            rot_seq[b, pl.ds(g * 64, 64), :] = moved_rot[b * 64 : b * 64 + 64]

    scale = (VDIM + ROPE) ** -0.5
    tile = 256

    def attend(b):
        keys = latent[b]
        rot_keys = jnp.concatenate([rotary[b], rotary[b]], axis=0)
        length = cache_len[b]
        for part in range(TB * HEADS // tile):
            rows = pl.ds(part * tile, tile)
            q = query_seq[b, rows, :]
            q_rot = rot_seq[b, rows, :]
            s = (dot_t(q, keys) + dot(q_rot, rot_keys)) * scale
            s_new = (dot_t(q, keys_new[...]) + dot_t(q_rot, rot_new[...])) * scale
            s = jnp.where(iota((tile, CACHE), 1) < length, s, -1e30)
            col = iota((tile, 128), 1)
            seen = jnp.logical_and(col // TB == b, col % TB <= iota((tile, 128), 0) % TB)
            s_new = jnp.where(seen, s_new, -1e30)
            top = jnp.maximum(
                jnp.max(s, axis=1, keepdims=True), jnp.max(s_new, axis=1, keepdims=True)
            )
            e = jnp.exp(s - top)
            e_new = jnp.exp(s_new - top)
            total = jnp.sum(e, axis=1, keepdims=True) + jnp.sum(e_new, axis=1, keepdims=True)
            mixed = dot(e.astype(BF16), keys) + dot(e_new.astype(BF16), keys_new[...])
            mixed = (mixed / total).astype(BF16)
            context[b, pl.ds(part * 2, 2)] = mixed.reshape(2, SIDE, 2, ROWS, KVL)

    def send(source, target, send_sem, recv_sem, to):
        pltpu.make_async_remote_copy(
            src_ref=source, dst_ref=target, send_sem=send_sem, recv_sem=recv_sem, device_id=to
        ).start()

    def scatter(b):
        arrived[b, 0, x, y] = context[b, x, y, core]

        @pl.loop(1, GROUP)
        def _(offset):
            to = (me + offset) % GROUP
            send(
                context.at[b, to // 8, to // 2 % SIDE, to % 2],
                arrived.at[b, (to + me) % 2, x, y],
                context_send.at[0],
                context_recv.at[b],
                {"expert": to},
            )

    load_latent.wait()
    load_rotary.wait()
    attend(0)
    pl.semaphore_wait(barrier, GROUP - 1 + (2 if sections > 1 else 0))
    scatter(0)

    @pl.loop(1, SEQ)
    def _(b):
        attend(b)
        scatter(b)

    def columns(c, piece):
        return pl.ds((piece * PARTS + c % PARTS) * WIDE, WIDE)

    def stack(upper, lower):
        count = upper.shape[0] // SHORT
        pair = [upper.reshape(count, SHORT, WIDE), lower.reshape(count, SHORT, WIDE)]
        return jnp.concatenate(pair, axis=1)

    def unstack(blocks):
        blocks = blocks.astype(F32)
        rows = blocks.shape[0] * SHORT
        return [
            blocks[:, SHORT * piece : SHORT * piece + SHORT].reshape(rows, WIDE)
            for piece in range(2)
        ]

    sent = pl.ds(0, (GROUP - 1) * ROWS)
    same_head = iota((512, 512), 0) % ROWS // TB == iota((512, 512), 1) // VDIM
    out_row = iota((64, 256), 0)
    in_row = iota((64, 256), 1)
    join = (
        (out_row // SHORT == in_row % 128 // ROWS)
        & (out_row % SHORT // TB == in_row // 128)
        & (out_row % TB == in_row % TB)
    ).astype(BF16)

    def raise_heads(batch):
        pair = range(2 * batch, 2 * batch + 2)
        for b in pair:
            settle(diagonal.at[b, sent], context_recv.at[b])
            product = dot(arrived[b].reshape(TB * HEADS, KVL), value_up[...])
            diagonal[b] = jnp.where(same_head, product, 0.0).astype(BF16)
        for g in range(4):
            group = jnp.concatenate([diagonal[b, pl.ds(g * 128, 128), :] for b in pair], axis=0)
            heads[batch, pl.ds(g * 64, 64), :] = dot(join, group).astype(BF16)

    def cross(which, c, partial):
        cross_out[which, c] = partial(c, 1).astype(BF16).reshape(HALF, WIDE)
        send(
            cross_out.at[which, c],
            cross_in.at[which, c],
            sum_send.at[which, 0],
            sum_recv.at[which, c, 0],
            {"expert": sibling},
        )

    def along_first(which, c, partial):
        mine = partial(c, 0)
        settle(cross_in.at[which, c], sum_recv.at[which, c, 0])
        theirs = cross_in[which, c].reshape(GROUP // 2, ROWS, WIDE).astype(F32)
        first_out[which, c] = (mine + theirs).astype(BF16).reshape(SIDE, SIDE, ROWS, WIDE)
        for half, step in ((0, 1), (1, SIDE - 1)):
            send(
                first_part(which, c, 2, half),
                first_in.at[which, c, 2, pl.ds(half * 2, 2)],
                sum_send.at[which, 1],
                sum_recv.at[which, c, 3],
                {"expert": ahead(c, step)},
            )
        for half, step in ((1, 1), (0, SIDE - 1)):
            to_neighbour(which, c, half, step)

    def line(c):
        return x if c % 2 == 0 else y

    def ahead(c, step):
        to = (line(c) + step) % SIDE
        return device(to, y) if c % 2 == 0 else device(x, to)

    def first_part(which, c, step, half):
        to = (line(c) + step) % SIDE
        pair = pl.ds(half * 2, 2)
        if c % 2 == 0:
            return first_out.at[which, c, to, pair]
        return first_out.at[which, c, pair, to]

    def to_neighbour(which, c, half, step):
        send(
            first_part(which, c, step, half),
            first_in.at[which, c, 0 if step == 1 else 1, pl.ds(half * 2, 2)],
            sum_send.at[which, 1],
            sum_recv.at[which, c, 1],
            {"expert": ahead(c, step)},
        )

    def relay_first(which, c):
        settle(first_in.at[which, c, 2], sum_recv.at[which, c, 3])
        for half, step in ((0, 1), (1, SIDE - 1)):
            part = first_part(which, c, step, half)
            through = first_in[which, c, 2, pl.ds(half * 2, 2)].astype(F32)
            part[...] = (part[...].astype(F32) + through).astype(BF16)
            to_neighbour(which, c, half, step)

    def along_second(which, c):
        settle(first_in.at[which, c, pl.ds(0, 2)], sum_recv.at[which, c, 1])
        if c % 2 == 0:
            rows = first_out[which, c, x].astype(F32)
        else:
            rows = first_out[which, c, :, y].astype(F32)
        for slot in range(2):
            rows = rows + first_in[which, c, slot].astype(F32)
        second_out[which, c] = rows.astype(BF16)
        for offset in range(1, SIDE):
            if c % 2 == 0:
                to = (y + offset) % SIDE
                where = device(x, to)
            else:
                to = (x + offset) % SIDE
                where = device(to, y)
            send(
                second_out.at[which, c, to],
                second_in.at[which, c, offset - 1],
                sum_send.at[which, 2],
                sum_recv.at[which, c, 2],
                {"expert": where},
            )

    def summed(which, c):
        settle(second_in.at[which, c], sum_recv.at[which, c, 2])
        rows = second_out[which, c, y if c % 2 == 0 else x].astype(F32)
        for slot in range(SIDE - 1):
            rows = rows + second_in[which, c, slot].astype(F32)
        return rows

    def chunks(batch):
        return range(batch * PARTS, batch * PARTS + PARTS)

    def projected(c, side):
        rows = heads[c // PARTS, pl.ds(side * HALF // 2, HALF // 2), :]
        return stack(*[dot(rows, out_weight[:, columns(c, piece)]) for piece in range(2)])

    def block(c, side, across):
        return gathered.at[c, side, across] if c % 2 == 0 else gathered.at[c, side, :, across]

    def normalise(batch):
        rows, squares = {}, 0.0
        half = slice(batch * SHORT, batch * SHORT + SHORT)
        for c in chunks(batch):
            left = [residual[:, columns(c, piece)].astype(F32)[half] for piece in range(2)]
            rows[c] = summed(0, c) + jnp.concatenate(left, axis=0)
            hidden[c] = rows[c]
            square = jnp.sum(rows[c] * rows[c], axis=1, keepdims=True)
            squares = squares + square[:SHORT] + square[SHORT:]
        factor = lax.rsqrt(squares * (1.0 / D) + 1e-06)
        factor = jnp.concatenate([factor, factor], axis=0)
        for c in chunks(batch):
            gain = jnp.concatenate(
                [
                    jnp.broadcast_to(norm_gain[:, columns(c, piece)], (SHORT, WIDE))
                    for piece in range(2)
                ],
                axis=0,
            )
            gathered[c, 0, x, y] = (rows[c] * factor * gain).astype(BF16)
            for offset in range(1, SIDE):
                to = (y if c % 2 == 0 else x) + offset
                send(
                    gathered.at[c, 0, x, y],
                    gathered.at[c, 0, x, y],
                    gather_send.at[0],
                    near_recv.at[c],
                    {"expert": device(x, to % SIDE) if c % 2 == 0 else device(to % SIDE, y)},
                )

    def to_sibling(c, across):
        send(
            block(c, 0, across),
            block(c, 1, across),
            gather_send.at[2],
            over_recv.at[c],
            {"expert": sibling},
        )

    def spread(c):
        settle(second_in.at[0, c], near_recv.at[c])
        here = line(c)
        for slot, step in enumerate(range(1, SIDE)):
            send(
                block(c, 0, here),
                block(c, 0, here),
                gather_send.at[1],
                far_recv.at[c, slot],
                {"expert": ahead(c, step)},
            )
        to_sibling(c, here)

    def add_units(c, side):
        pieces = unstack(gathered[c, side].reshape(GROUP // 2, ROWS, WIDE))
        product = 0.0
        for piece in range(2):
            product = product + dot(pieces[piece].astype(BF16), gate_up[columns(c, piece), :])
        if c % PARTS == 0:
            hidden_units[c // PARTS, side] = product
        else:
            hidden_units[c // PARTS, side] = hidden_units[c // PARTS, side] + product

    def pass_on(c):
        here = line(c)
        for step in range(1, SIDE):
            settle(block(c, 0, here), far_recv.at[c, step - 1])
            to_sibling(c, (here + SIDE - step) % SIDE)
        add_units(c, 0)

    def take_over(c):
        settle(gathered.at[c, 1], over_recv.at[c])
        add_units(c, 1)

    def activate(batch, side):
        gate_value = hidden_units[batch, side, :, pl.ds(0, FF_DEV)]
        up_value = hidden_units[batch, side, :, pl.ds(FF_DEV, FF_DEV)]
        activation[batch, side] = (
            gate_value * jax.nn.sigmoid(gate_value) * up_value
        ).astype(BF16)

    def expert_share(c, side):
        batch = c // PARTS
        weight = chosen[pl.ds(side * HALF, HALF), :].reshape(GROUP // 2, ROWS, 128)
        weight = weight[:, batch * SHORT : batch * SHORT + SHORT].reshape(HALF // 2, 128)
        weight = jnp.concatenate([weight] * (WIDE // 128), axis=1)
        rows = activation[batch, side]
        return stack(*[dot(rows, down[:, columns(c, piece)]) * weight for piece in range(2)])

    def finish(c):
        rows = hidden[c] + summed(1, c)
        if c // PARTS == 0:
            mixed_rows[c] = rows
            return
        before = mixed_rows[c % PARTS]
        for piece in range(2):
            half = slice(piece * SHORT, piece * SHORT + SHORT)
            slot = c % PARTS * 2 + piece
            handed[slot] = jnp.concatenate([before[half], rows[half]], axis=0).astype(BF16)
            target = out_hbm.at[:, columns(c, piece)]
            if sections > 1:
                send(
                    handed.at[slot],
                    target,
                    hand_sem.at[0],
                    hand_sem.at[1],
                    {"section": (section + 1) % sections},
                )
            else:
                load(handed.at[slot], target, hand_sem.at[0]).wait()

    settle(value_up, load_sem.at[4])

    def stage_heads(batch):
        raise_heads(batch)
        if batch == 0:
            load_out.wait()
        for c in chunks(batch):
            cross(0, c, projected)

    def stage_first(batch):
        for c in chunks(batch):
            along_first(0, c, projected)

    def stage_relay(batch):
        for c in chunks(batch):
            relay_first(0, c)

    def stage_second(batch):
        for c in chunks(batch):
            along_second(0, c)

    def stage_norm(batch):
        if batch == 0:
            load_res.wait()
        normalise(batch)

    def stage_spread(batch):
        for c in chunks(batch):
            spread(c)

    def stage_pass(batch):
        if batch == 0:
            settle(gate_up, load_sem.at[7])
        for c in chunks(batch):
            pass_on(c)

    def stage_units(batch):
        for c in chunks(batch):
            take_over(c)
        if batch == 0:
            load_down.wait()
        activate(batch, 1)
        for c in chunks(batch):
            cross(1, c, expert_share)

    def stage_shares(batch):
        activate(batch, 0)
        for c in chunks(batch):
            along_first(1, c, expert_share)

    def stage_through(batch):
        for c in chunks(batch):
            relay_first(1, c)

    def stage_last(batch):
        for c in chunks(batch):
            along_second(1, c)

    def stage_finish(batch):
        for c in chunks(batch):
            finish(c)

    stage_heads(0)
    stage_first(0)
    stage_heads(1)
    stage_relay(0)
    stage_first(1)
    stage_second(0)
    stage_relay(1)
    stage_norm(0)
    stage_second(1)
    stage_spread(0)
    stage_norm(1)
    stage_spread(1)
    stage_pass(0)
    stage_units(0)
    stage_shares(0)
    stage_pass(1)
    stage_units(1)
    stage_through(0)
    stage_shares(1)
    stage_last(0)
    stage_through(1)
    stage_finish(0)
    stage_last(1)
    stage_finish(1)

    settle(diagonal.at[:, sent], context_send.at[0])
    for which in range(2):
        settle(cross_out.at[which], sum_send.at[which, 0])
        settle(first_in.at[which], sum_send.at[which, 1])
        settle(second_in.at[which], sum_send.at[which, 2])
    settle(second_in.at[0], gather_send.at[0])
    settle(first_in.at[0], gather_send.at[1])
    settle(gathered.at[:, 0], gather_send.at[2])
    if sections > 1:
        settle(handed, hand_sem.at[0])
        settle(handed, hand_sem.at[1])


def local(
    residual,
    query_latent,
    query_rotary,
    cache_latent,
    cache_rotary,
    new_latent,
    new_rotary,
    cache_len,
    route_ids,
    routing_weight,
    norm_gain,
    value_up_matrix,
    out_weight,
    gate_weight,
    up_weight,
    down_weight,
):
    sections = lax.axis_size("section")
    far = pl.BlockSpec(memory_space=pl.ANY)
    near = pl.BlockSpec(memory_space=pltpu.VMEM)
    scalar = pl.BlockSpec(memory_space=pltpu.SMEM)
    dma = pltpu.SemaphoreType.DMA
    scratch = [
        pltpu.VMEM((ROWS, D), BF16),
        pltpu.VMEM((ROWS, HEADS * KVL), BF16),
        pltpu.VMEM((ROWS, HEADS * ROPE), BF16),
        pltpu.VMEM((SEQ, CACHE, KVL), BF16),
        pltpu.VMEM((SEQ, ROPE, CACHE), BF16),
        pltpu.VMEM((KVL, 4 * VDIM), BF16),
        pltpu.VMEM((4 * VDIM, D), BF16),
        pltpu.VMEM((D, 2 * FF_DEV), BF16),
        pltpu.VMEM((FF_DEV, D), BF16),
        pltpu.VMEM((SEQ, TB * HEADS, KVL), BF16),
        pltpu.VMEM((SEQ, TB * HEADS, 128), BF16),
        pltpu.VMEM((128, KVL), BF16),
        pltpu.VMEM((128, 128), BF16),
        pltpu.VMEM((SEQ, SIDE, SIDE, 2, ROWS, KVL), BF16),
        pltpu.VMEM((SEQ, 2, SIDE, SIDE, ROWS, KVL), BF16),
        pltpu.VMEM((SEQ, TB * HEADS, KVL), BF16),
        pltpu.VMEM((BATCHES, HALF, 4 * VDIM), BF16),
        pltpu.VMEM((GROUP * ROWS, 128), F32),
        pltpu.VMEM((GROUP * ROWS, 128), F32),
        pltpu.VMEM((2, CHUNKS, HALF, WIDE), BF16),
        pltpu.VMEM((2, CHUNKS, HALF, WIDE), BF16),
        pltpu.VMEM((2, CHUNKS, SIDE, SIDE, ROWS, WIDE), BF16),
        pltpu.VMEM((2, CHUNKS, SIDE - 1, SIDE, ROWS, WIDE), BF16),
        pltpu.VMEM((2, CHUNKS, SIDE, ROWS, WIDE), BF16),
        pltpu.VMEM((2, CHUNKS, SIDE - 1, ROWS, WIDE), BF16),
        pltpu.VMEM((CHUNKS, ROWS, WIDE), F32),
        pltpu.VMEM((CHUNKS, 2, SIDE, SIDE, ROWS, WIDE), BF16),
        pltpu.VMEM((BATCHES, 2, HALF // 2, 2 * FF_DEV), F32),
        pltpu.VMEM((BATCHES, 2, HALF // 2, FF_DEV), BF16),
        pltpu.VMEM((PARTS, ROWS, WIDE), F32),
        pltpu.VMEM((CHUNKS, ROWS, WIDE), BF16),
        dma((9,)),
        dma((1,)),
        dma((SEQ,)),
        dma((2, 3)),
        dma((2, CHUNKS, 4)),
        dma((3,)),
        dma((CHUNKS,)),
        dma((CHUNKS, SIDE - 1)),
        dma((CHUNKS,)),
        dma((2,)),
    ]

    def kernel(*refs):
        layer_kernel(sections, *refs)

    return pl.pallas_call(
        kernel,
        out_shape=jax.ShapeDtypeStruct((ROWS, D), BF16),
        in_specs=[far] * 5 + [near, near, scalar, near, near, near] + [far] * 5,
        out_specs=far,
        scratch_shapes=scratch,
        compiler_params=pltpu.CompilerParams(
            collective_id=0, has_side_effects=True, vmem_limit_bytes=60 * 1024 * 1024
        ),
        name="layer",
    )(
        residual,
        query_latent,
        query_rotary,
        cache_latent,
        cache_rotary,
        new_latent,
        new_rotary.T,
        cache_len,
        route_ids.T,
        routing_weight.T,
        norm_gain,
        value_up_matrix,
        out_weight,
        gate_weight,
        up_weight,
        down_weight,
    )


def solution(mesh):
    rows = P(("section", "expert"), None)
    placed = (
        rows,
        rows,
        rows,
        P(("section", "expert"), None, None),
        P(("section", "expert"), None, None),
        rows,
        P(None, ("section", "expert")),
        P(("section", "expert")),
        P("section", None),
        P("section", None),
        P("section", None),
        P("section", "expert", None, None),
        P("section", "expert", None),
        P("section", None, "expert"),
        P("section", None, "expert"),
        P("section", "expert", None),
    )
    return jax.shard_map(local, mesh=mesh, in_specs=placed, out_specs=rows, check_vma=False)
```

```python
import jax
import jax.numpy as jnp
from jax import lax
from jax.experimental import pallas as pl
from jax.experimental.pallas import tpu as pltpu
from jax.sharding import PartitionSpec as P

D = 3584
KVL = 512
ROPE = 64
VDIM = 128
HEADS = 128
TB = 4
SEQ = 4
ROWS = 16
CACHE = 512
FF_DEV = 256
SIDE = 4
GROUP = 32
BATCHES = 2
PARTS = 4
CHUNKS = BATCHES * PARTS
WIDTHS = (512, 384)
HALF = GROUP * ROWS // 2
SHORT = ROWS // BATCHES

BF16 = jnp.bfloat16
F32 = jnp.float32

FARTHEST_FIRST = sorted(
    [(i, j, k) for i in range(SIDE) for j in range(SIDE) for k in range(2) if i + j + k],
    key=lambda step: -min(step[0], SIDE - step[0]) - min(step[1], SIDE - step[1]),
)


def dot(a, b):
    return lax.dot_general(a, b, (((1,), (0,)), ((), ())), preferred_element_type=F32)


def dot_t(a, b):
    return lax.dot_general(a, b, (((1,), (1,)), ((), ())), preferred_element_type=F32)


def iota(shape, dim):
    return lax.broadcasted_iota(jnp.int32, shape, dim)


def kind(c):
    return c % PARTS // 2


def width(c):
    return WIDTHS[kind(c)]


class Chunked:
    def __init__(self, pair, place):
        self.pair, self.place = pair, place

    def find(self, index):
        index = index if isinstance(index, tuple) else (index,)
        c = index[self.place]
        slot = c // PARTS * 2 + c % 2
        return kind(c), index[: self.place] + (slot,) + index[self.place + 1 :]

    def __getitem__(self, index):
        which, index = self.find(index)
        return self.pair[which][index]

    def __setitem__(self, index, value):
        which, index = self.find(index)
        self.pair[which][index] = value

    @property
    def at(self):
        return Chunked([ref.at for ref in self.pair], self.place)


def layer_kernel(
    sections,
    residual_hbm,
    query_hbm,
    query_rot_hbm,
    latent_hbm,
    rotary_hbm,
    new_latent,
    new_rotary,
    cache_len,
    route_ids,
    routing_weight,
    norm_gain,
    value_up_hbm,
    out_weight_hbm,
    gate_hbm,
    up_hbm,
    down_hbm,
    out_hbm,
    residual,
    query,
    query_rot,
    latent,
    rotary,
    value_up,
    out_weight,
    gate_up,
    down,
    query_seq,
    rot_seq,
    keys_new,
    rot_new,
    context,
    arrived,
    diagonal,
    heads,
    chosen_all,
    chosen,
    cross_out_wide,
    cross_out_narrow,
    cross_in_wide,
    cross_in_narrow,
    first_out_wide,
    first_out_narrow,
    first_in_wide,
    first_in_narrow,
    second_out_wide,
    second_out_narrow,
    second_in_wide,
    second_in_narrow,
    hidden_wide,
    hidden_narrow,
    gathered_wide,
    gathered_narrow,
    hidden_units,
    activation,
    mixed_rows_wide,
    mixed_rows_narrow,
    handed_wide,
    handed_narrow,
    load_sem,
    context_send,
    context_recv,
    sum_send,
    sum_recv,
    gather_send,
    near_recv,
    far_recv,
    over_recv,
    hand_sem,
):
    cross_out = Chunked((cross_out_wide, cross_out_narrow), 1)
    cross_in = Chunked((cross_in_wide, cross_in_narrow), 1)
    first_out = Chunked((first_out_wide, first_out_narrow), 1)
    first_in = Chunked((first_in_wide, first_in_narrow), 1)
    second_out = Chunked((second_out_wide, second_out_narrow), 1)
    second_in = Chunked((second_in_wide, second_in_narrow), 1)
    hidden = Chunked((hidden_wide, hidden_narrow), 0)
    gathered = Chunked((gathered_wide, gathered_narrow), 0)
    mixed_rows = Chunked((mixed_rows_wide, mixed_rows_narrow), 0)
    handed = Chunked((handed_wide, handed_narrow), 0)
    section = lax.axis_index("section")
    me = lax.axis_index("expert")
    core = me % 2
    chip = me // 2
    x = chip // SIDE
    y = chip % SIDE
    sibling = chip * 2 + 1 - core

    def device(chip_x, chip_y):
        return (chip_x * SIDE + chip_y) * 2 + core

    barrier = pltpu.get_barrier_semaphore()

    @pl.loop(1, GROUP)
    def _(offset):
        pl.semaphore_signal(barrier, inc=1, device_id={"expert": (me + offset) % GROUP})

    if sections > 1:
        pl.semaphore_signal(barrier, inc=1, device_id={"section": (section + 1) % sections})
        pl.semaphore_signal(
            barrier, inc=1, device_id={"section": (section + sections - 1) % sections}
        )

    def load(source, target, sem):
        copy = pltpu.make_async_copy(source, target, sem)
        copy.start()
        return copy

    load_query = load(query_hbm, query, load_sem.at[0])
    load_rot = load(query_rot_hbm, query_rot, load_sem.at[1])
    load_latent = load(latent_hbm, latent, load_sem.at[2])
    load_rotary = load(rotary_hbm, rotary, load_sem.at[3])
    for j in range(4):
        load(value_up_hbm.at[0, j], value_up.at[:, pl.ds(j * VDIM, VDIM)], load_sem.at[4])
    load_out = load(out_weight_hbm.at[0], out_weight, load_sem.at[5])
    load_res = load(residual_hbm, residual, load_sem.at[6])
    load(gate_hbm.at[0], gate_up.at[:, pl.ds(0, FF_DEV)], load_sem.at[7])
    load(up_hbm.at[0], gate_up.at[:, pl.ds(FF_DEV, FF_DEV)], load_sem.at[7])
    load_down = load(down_hbm.at[0], down, load_sem.at[8])

    def settle(like, sem):
        pltpu.make_async_copy(like, like, sem).wait()

    keys_new[...] = jnp.zeros_like(keys_new)
    keys_new[pl.ds(0, ROWS), :] = new_latent[...]
    twice = (iota((ROPE, 128), 1) % ROPE == iota((ROPE, 128), 0)).astype(BF16)
    rot_new[...] = jnp.zeros_like(rot_new)
    rot_new[pl.ds(0, ROWS), :] = dot(new_rotary[...], twice).astype(BF16)

    expert = x
    weight_row = jnp.sum(
        jnp.where(route_ids[...] == expert, routing_weight[...], 0.0), axis=0, keepdims=True
    )
    chosen_all[...] = jnp.broadcast_to(weight_row, (128, GROUP * ROWS)).T
    for side in range(2):
        for place in range(GROUP // 2):
            source = (place * 2 + (core + side) % 2) * ROWS
            chosen[pl.ds((side * 16 + place) * ROWS, ROWS), :] = chosen_all[
                pl.ds(pl.multiple_of(source, ROWS), ROWS), :
            ]

    row_to = iota((256, 256), 0)
    row_from = iota((256, 256), 1)
    permute = (
        row_from == (row_to % 64) // TB * ROWS + row_to // 64 * TB + row_to % TB
    ).astype(BF16)
    low = iota((ROWS, 128), 1) < ROPE
    load_query.wait()
    load_rot.wait()
    for g in range(8):
        pieces, rot_pieces = [], []
        for h in range(g * 16, g * 16 + 16):
            pieces.append(query[:, pl.ds(h * KVL, KVL)])
            pair = query_rot[:, pl.ds(h // 2 * 128, 128)]
            keep = low if h % 2 == 0 else jnp.logical_not(low)
            rot_pieces.append(jnp.where(keep, pair, jnp.zeros_like(pair)))
        moved = dot(permute, jnp.concatenate(pieces, axis=0)).astype(BF16)
        moved_rot = dot(permute, jnp.concatenate(rot_pieces, axis=0)).astype(BF16)
        for b in range(SEQ):
            query_seq[b, pl.ds(g * 64, 64), :] = moved[b * 64 : b * 64 + 64]
            rot_seq[b, pl.ds(g * 64, 64), :] = moved_rot[b * 64 : b * 64 + 64]

    scale = (VDIM + ROPE) ** -0.5
    tile = 256

    def attend(b):
        keys = latent[b]
        rot_keys = jnp.concatenate([rotary[b], rotary[b]], axis=0)
        length = cache_len[b]
        for part in range(TB * HEADS // tile):
            rows = pl.ds(part * tile, tile)
            q = query_seq[b, rows, :]
            q_rot = rot_seq[b, rows, :]
            s = (dot_t(q, keys) + dot(q_rot, rot_keys)) * scale
            s_new = (dot_t(q, keys_new[...]) + dot_t(q_rot, rot_new[...])) * scale
            s = jnp.where(iota((tile, CACHE), 1) < length, s, -1e30)
            col = iota((tile, 128), 1)
            seen = jnp.logical_and(col // TB == b, col % TB <= iota((tile, 128), 0) % TB)
            s_new = jnp.where(seen, s_new, -1e30)
            top = jnp.maximum(
                jnp.max(s, axis=1, keepdims=True), jnp.max(s_new, axis=1, keepdims=True)
            )
            e = jnp.exp(s - top)
            e_new = jnp.exp(s_new - top)
            total = jnp.sum(e, axis=1, keepdims=True) + jnp.sum(e_new, axis=1, keepdims=True)
            mixed = dot(e.astype(BF16), keys) + dot(e_new.astype(BF16), keys_new[...])
            mixed = (mixed / total).astype(BF16)
            context[b, pl.ds(part * 2, 2)] = mixed.reshape(2, SIDE, 2, ROWS, KVL)

    def send(source, target, send_sem, recv_sem, to):
        pltpu.make_async_remote_copy(
            src_ref=source, dst_ref=target, send_sem=send_sem, recv_sem=recv_sem, device_id=to
        ).start()

    def scatter(b):
        arrived[b, 0, x, y] = context[b, x, y, core]

        for step_x, step_y, other in FARTHEST_FIRST:
            to_x, to_y, there = (x + step_x) % SIDE, (y + step_y) % SIDE, (core + other) % 2
            send(
                context.at[b, to_x, to_y, there],
                arrived.at[b, other, x, y],
                context_send.at[0],
                context_recv.at[b],
                {"expert": (to_x * SIDE + to_y) * 2 + there},
            )

    load_latent.wait()
    load_rotary.wait()
    attend(0)
    pl.semaphore_wait(barrier, GROUP - 1 + (2 if sections > 1 else 0))
    scatter(0)

    @pl.loop(1, SEQ)
    def _(b):
        attend(b)
        scatter(b)

    def columns(c, piece):
        start = piece * (D // 2) + c % 2 * (D // 4) + kind(c) * WIDTHS[0]
        return pl.ds(start, width(c))

    def stack(upper, lower):
        count = upper.shape[0] // SHORT
        pair = [part.reshape(count, SHORT, part.shape[1]) for part in (upper, lower)]
        return jnp.concatenate(pair, axis=1)

    def unstack(blocks):
        blocks = blocks.astype(F32)
        rows = blocks.shape[0] * SHORT
        return [
            blocks[:, SHORT * piece : SHORT * piece + SHORT].reshape(rows, blocks.shape[2])
            for piece in range(2)
        ]

    sent = pl.ds(0, (GROUP - 1) * ROWS)
    same_head = iota((512, 512), 0) % ROWS // TB == iota((512, 512), 1) // VDIM
    out_row = iota((64, 256), 0)
    in_row = iota((64, 256), 1)
    join = (
        (out_row // SHORT == in_row % 128 // ROWS)
        & (out_row % SHORT // TB == in_row // 128)
        & (out_row % TB == in_row % TB)
    ).astype(BF16)

    def raise_heads(batch):
        pair = range(2 * batch, 2 * batch + 2)
        for b in pair:
            settle(diagonal.at[b, sent], context_recv.at[b])
            product = dot(arrived[b].reshape(TB * HEADS, KVL), value_up[...])
            diagonal[b] = jnp.where(same_head, product, 0.0).astype(BF16)
        for g in range(4):
            group = jnp.concatenate([diagonal[b, pl.ds(g * 128, 128), :] for b in pair], axis=0)
            heads[batch, pl.ds(g * 64, 64), :] = dot(join, group).astype(BF16)

    def cross(which, c, partial):
        cross_out[which, c] = partial(c, 1).astype(BF16).reshape(HALF, width(c))
        send(
            cross_out.at[which, c],
            cross_in.at[which, c],
            sum_send.at[which, 0, kind(c)],
            sum_recv.at[which, c, 0],
            {"expert": sibling},
        )

    def along_first(which, c, partial):
        mine = partial(c, 0)
        settle(cross_in.at[which, c], sum_recv.at[which, c, 0])
        theirs = cross_in[which, c].reshape(GROUP // 2, ROWS, width(c)).astype(F32)
        first_out[which, c] = (mine + theirs).astype(BF16).reshape(SIDE, SIDE, ROWS, width(c))
        for half, step in ((0, 1), (1, SIDE - 1)):
            send(
                first_part(which, c, 2, half),
                first_in.at[which, c, 2, pl.ds(half * 2, 2)],
                sum_send.at[which, 1, kind(c)],
                sum_recv.at[which, c, 3],
                {"expert": ahead(c, step)},
            )
        for half, step in ((1, 1), (0, SIDE - 1)):
            to_neighbour(which, c, half, step)

    def line(c):
        return x if c % 2 == 0 else y

    def ahead(c, step):
        to = (line(c) + step) % SIDE
        return device(to, y) if c % 2 == 0 else device(x, to)

    def first_part(which, c, step, half):
        to = (line(c) + step) % SIDE
        pair = pl.ds(half * 2, 2)
        if c % 2 == 0:
            return first_out.at[which, c, to, pair]
        return first_out.at[which, c, pair, to]

    def to_neighbour(which, c, half, step):
        send(
            first_part(which, c, step, half),
            first_in.at[which, c, 0 if step == 1 else 1, pl.ds(half * 2, 2)],
            sum_send.at[which, 1, kind(c)],
            sum_recv.at[which, c, 1],
            {"expert": ahead(c, step)},
        )

    def relay_first(which, c):
        settle(first_in.at[which, c, 2], sum_recv.at[which, c, 3])
        for half, step in ((0, 1), (1, SIDE - 1)):
            part = first_part(which, c, step, half)
            through = first_in[which, c, 2, pl.ds(half * 2, 2)].astype(F32)
            part[...] = (part[...].astype(F32) + through).astype(BF16)
            to_neighbour(which, c, half, step)

    def along_second(which, c):
        settle(first_in.at[which, c, pl.ds(0, 2)], sum_recv.at[which, c, 1])
        if c % 2 == 0:
            rows = first_out[which, c, x].astype(F32)
        else:
            rows = first_out[which, c, :, y].astype(F32)
        for slot in range(2):
            rows = rows + first_in[which, c, slot].astype(F32)
        second_out[which, c] = rows.astype(BF16)
        for offset in range(1, SIDE):
            if c % 2 == 0:
                to = (y + offset) % SIDE
                where = device(x, to)
            else:
                to = (x + offset) % SIDE
                where = device(to, y)
            send(
                second_out.at[which, c, to],
                second_in.at[which, c, offset - 1],
                sum_send.at[which, 2, kind(c)],
                sum_recv.at[which, c, 2],
                {"expert": where},
            )

    def summed(which, c):
        settle(second_in.at[which, c], sum_recv.at[which, c, 2])
        rows = second_out[which, c, y if c % 2 == 0 else x].astype(F32)
        for slot in range(SIDE - 1):
            rows = rows + second_in[which, c, slot].astype(F32)
        return rows

    def chunks(batch):
        return range(batch * PARTS, batch * PARTS + PARTS)

    def projected(c, side):
        rows = heads[c // PARTS, pl.ds(side * HALF // 2, HALF // 2), :]
        return stack(*[dot(rows, out_weight[:, columns(c, piece)]) for piece in range(2)])

    def block(c, side, across):
        return gathered.at[c, side, across] if c % 2 == 0 else gathered.at[c, side, :, across]

    def normalise(batch):
        rows, squares = {}, 0.0
        half = slice(batch * SHORT, batch * SHORT + SHORT)
        for c in chunks(batch):
            left = [residual[:, columns(c, piece)].astype(F32)[half] for piece in range(2)]
            rows[c] = summed(0, c) + jnp.concatenate(left, axis=0)
            hidden[c] = rows[c]
            square = jnp.sum(rows[c] * rows[c], axis=1, keepdims=True)
            squares = squares + square[:SHORT] + square[SHORT:]
        factor = lax.rsqrt(squares * (1.0 / D) + 1e-06)
        factor = jnp.concatenate([factor, factor], axis=0)
        for c in chunks(batch):
            gain = jnp.concatenate(
                [
                    jnp.broadcast_to(norm_gain[:, columns(c, piece)], (SHORT, width(c)))
                    for piece in range(2)
                ],
                axis=0,
            )
            gathered[c, 0, x, y] = (rows[c] * factor * gain).astype(BF16)
            for offset in range(1, SIDE):
                to = (y if c % 2 == 0 else x) + offset
                send(
                    gathered.at[c, 0, x, y],
                    gathered.at[c, 0, x, y],
                    gather_send.at[0, kind(c)],
                    near_recv.at[c],
                    {"expert": device(x, to % SIDE) if c % 2 == 0 else device(to % SIDE, y)},
                )

    def to_sibling(c, across):
        send(
            block(c, 0, across),
            block(c, 1, across),
            gather_send.at[2, kind(c)],
            over_recv.at[c],
            {"expert": sibling},
        )

    def spread(c):
        settle(second_in.at[0, c], near_recv.at[c])
        here = line(c)
        for slot, step in enumerate(range(1, SIDE)):
            send(
                block(c, 0, here),
                block(c, 0, here),
                gather_send.at[1, kind(c)],
                far_recv.at[c, slot],
                {"expert": ahead(c, step)},
            )
        to_sibling(c, here)

    def add_units(c, side):
        pieces = unstack(gathered[c, side].reshape(GROUP // 2, ROWS, width(c)))
        product = 0.0
        for piece in range(2):
            product = product + dot(pieces[piece].astype(BF16), gate_up[columns(c, piece), :])
        if c % PARTS == 0:
            hidden_units[c // PARTS, side] = product
        else:
            hidden_units[c // PARTS, side] = hidden_units[c // PARTS, side] + product

    def pass_on(c):
        here = line(c)
        for step in range(1, SIDE):
            settle(block(c, 0, here), far_recv.at[c, step - 1])
            to_sibling(c, (here + SIDE - step) % SIDE)
        add_units(c, 0)

    def take_over(c):
        settle(gathered.at[c, 1], over_recv.at[c])
        add_units(c, 1)

    def activate(batch, side):
        gate_value = hidden_units[batch, side, :, pl.ds(0, FF_DEV)]
        up_value = hidden_units[batch, side, :, pl.ds(FF_DEV, FF_DEV)]
        activation[batch, side] = (
            gate_value * jax.nn.sigmoid(gate_value) * up_value
        ).astype(BF16)

    def expert_share(c, side):
        batch = c // PARTS
        weight = chosen[pl.ds(side * HALF, HALF), :].reshape(GROUP // 2, ROWS, 128)
        weight = weight[:, batch * SHORT : batch * SHORT + SHORT].reshape(HALF // 2, 128)
        weight = jnp.concatenate([weight] * (width(c) // 128), axis=1)
        rows = activation[batch, side]
        return stack(*[dot(rows, down[:, columns(c, piece)]) * weight for piece in range(2)])

    def finish(c):
        rows = hidden[c] + summed(1, c)
        if c // PARTS == 0:
            mixed_rows[c] = rows
            return
        before = mixed_rows[c % PARTS]
        for piece in range(2):
            half = slice(piece * SHORT, piece * SHORT + SHORT)
            handed[c % PARTS, piece] = jnp.concatenate([before[half], rows[half]], axis=0).astype(BF16)
            target = out_hbm.at[:, columns(c, piece)]
            if sections > 1:
                send(
                    handed.at[c % PARTS, piece],
                    target,
                    hand_sem.at[0, kind(c)],
                    hand_sem.at[1, kind(c)],
                    {"section": (section + 1) % sections},
                )
            else:
                load(handed.at[c % PARTS, piece], target, hand_sem.at[0, kind(c)]).wait()

    settle(value_up, load_sem.at[4])

    def stage_heads(batch):
        raise_heads(batch)
        if batch == 0:
            load_out.wait()
        for c in chunks(batch):
            cross(0, c, projected)

    def stage_first(batch):
        for c in chunks(batch):
            along_first(0, c, projected)

    def stage_relay(batch):
        for c in chunks(batch):
            relay_first(0, c)

    def stage_second(batch):
        for c in chunks(batch):
            along_second(0, c)

    def stage_norm(batch):
        if batch == 0:
            load_res.wait()
        normalise(batch)

    def stage_spread(batch):
        for c in chunks(batch):
            spread(c)

    def stage_pass(batch):
        if batch == 0:
            settle(gate_up, load_sem.at[7])
        for c in chunks(batch):
            pass_on(c)

    def stage_units(batch):
        for c in chunks(batch):
            take_over(c)
        if batch == 0:
            load_down.wait()
        activate(batch, 1)
        for c in chunks(batch):
            cross(1, c, expert_share)

    def stage_shares(batch):
        activate(batch, 0)
        for c in chunks(batch):
            along_first(1, c, expert_share)

    def stage_through(batch):
        for c in chunks(batch):
            relay_first(1, c)

    def stage_last(batch):
        for c in chunks(batch):
            along_second(1, c)

    def stage_finish(batch):
        for c in chunks(batch):
            finish(c)

    stage_heads(0)
    stage_first(0)
    stage_heads(1)
    stage_relay(0)
    stage_first(1)
    stage_second(0)
    stage_relay(1)
    stage_norm(0)
    stage_second(1)
    stage_spread(0)
    stage_norm(1)
    stage_pass(0)
    stage_spread(1)
    stage_units(0)
    stage_shares(0)
    stage_pass(1)
    stage_units(1)
    stage_through(0)
    stage_shares(1)
    stage_last(0)
    stage_through(1)
    stage_last(1)
    stage_finish(0)
    stage_finish(1)

    settle(diagonal.at[:, sent], context_send.at[0])
    for size in range(2):
        for which in range(2):
            settle(cross_out.pair[size].at[which], sum_send.at[which, 0, size])
            settle(first_in.pair[size].at[which], sum_send.at[which, 1, size])
            settle(second_in.pair[size].at[which], sum_send.at[which, 2, size])
        settle(second_in.pair[size].at[0], gather_send.at[0, size])
        settle(first_in.pair[size].at[0], gather_send.at[1, size])
        settle(gathered.pair[size].at[:, 0], gather_send.at[2, size])
        if sections > 1:
            settle(handed.pair[size], hand_sem.at[0, size])
            settle(handed.pair[size], hand_sem.at[1, size])


def local(
    residual,
    query_latent,
    query_rotary,
    cache_latent,
    cache_rotary,
    new_latent,
    new_rotary,
    cache_len,
    route_ids,
    routing_weight,
    norm_gain,
    value_up_matrix,
    out_weight,
    gate_weight,
    up_weight,
    down_weight,
):
    sections = lax.axis_size("section")
    far = pl.BlockSpec(memory_space=pl.ANY)
    near = pl.BlockSpec(memory_space=pltpu.VMEM)
    scalar = pl.BlockSpec(memory_space=pltpu.SMEM)
    dma = pltpu.SemaphoreType.DMA
    scratch = [
        pltpu.VMEM((ROWS, D), BF16),
        pltpu.VMEM((ROWS, HEADS * KVL), BF16),
        pltpu.VMEM((ROWS, HEADS * ROPE), BF16),
        pltpu.VMEM((SEQ, CACHE, KVL), BF16),
        pltpu.VMEM((SEQ, ROPE, CACHE), BF16),
        pltpu.VMEM((KVL, 4 * VDIM), BF16),
        pltpu.VMEM((4 * VDIM, D), BF16),
        pltpu.VMEM((D, 2 * FF_DEV), BF16),
        pltpu.VMEM((FF_DEV, D), BF16),
        pltpu.VMEM((SEQ, TB * HEADS, KVL), BF16),
        pltpu.VMEM((SEQ, TB * HEADS, 128), BF16),
        pltpu.VMEM((128, KVL), BF16),
        pltpu.VMEM((128, 128), BF16),
        pltpu.VMEM((SEQ, SIDE, SIDE, 2, ROWS, KVL), BF16),
        pltpu.VMEM((SEQ, 2, SIDE, SIDE, ROWS, KVL), BF16),
        pltpu.VMEM((SEQ, TB * HEADS, KVL), BF16),
        pltpu.VMEM((BATCHES, HALF, 4 * VDIM), BF16),
        pltpu.VMEM((GROUP * ROWS, 128), F32),
        pltpu.VMEM((GROUP * ROWS, 128), F32),
        pltpu.VMEM((2, 2 * BATCHES, HALF, WIDTHS[0]), BF16),
        pltpu.VMEM((2, 2 * BATCHES, HALF, WIDTHS[1]), BF16),
        pltpu.VMEM((2, 2 * BATCHES, HALF, WIDTHS[0]), BF16),
        pltpu.VMEM((2, 2 * BATCHES, HALF, WIDTHS[1]), BF16),
        pltpu.VMEM((2, 2 * BATCHES, SIDE, SIDE, ROWS, WIDTHS[0]), BF16),
        pltpu.VMEM((2, 2 * BATCHES, SIDE, SIDE, ROWS, WIDTHS[1]), BF16),
        pltpu.VMEM((2, 2 * BATCHES, SIDE - 1, SIDE, ROWS, WIDTHS[0]), BF16),
        pltpu.VMEM((2, 2 * BATCHES, SIDE - 1, SIDE, ROWS, WIDTHS[1]), BF16),
        pltpu.VMEM((2, 2 * BATCHES, SIDE, ROWS, WIDTHS[0]), BF16),
        pltpu.VMEM((2, 2 * BATCHES, SIDE, ROWS, WIDTHS[1]), BF16),
        pltpu.VMEM((2, 2 * BATCHES, SIDE - 1, ROWS, WIDTHS[0]), BF16),
        pltpu.VMEM((2, 2 * BATCHES, SIDE - 1, ROWS, WIDTHS[1]), BF16),
        pltpu.VMEM((2 * BATCHES, ROWS, WIDTHS[0]), F32),
        pltpu.VMEM((2 * BATCHES, ROWS, WIDTHS[1]), F32),
        pltpu.VMEM((2 * BATCHES, 2, SIDE, SIDE, ROWS, WIDTHS[0]), BF16),
        pltpu.VMEM((2 * BATCHES, 2, SIDE, SIDE, ROWS, WIDTHS[1]), BF16),
        pltpu.VMEM((BATCHES, 2, HALF // 2, 2 * FF_DEV), F32),
        pltpu.VMEM((BATCHES, 2, HALF // 2, FF_DEV), BF16),
        pltpu.VMEM((2, ROWS, WIDTHS[0]), F32),
        pltpu.VMEM((2, ROWS, WIDTHS[1]), F32),
        pltpu.VMEM((2, 2, ROWS, WIDTHS[0]), BF16),
        pltpu.VMEM((2, 2, ROWS, WIDTHS[1]), BF16),
        dma((9,)),
        dma((1,)),
        dma((SEQ,)),
        dma((2, 3, 2)),
        dma((2, CHUNKS, 4)),
        dma((3, 2)),
        dma((CHUNKS,)),
        dma((CHUNKS, SIDE - 1)),
        dma((CHUNKS,)),
        dma((2, 2)),
    ]

    def kernel(*refs):
        layer_kernel(sections, *refs)

    return pl.pallas_call(
        kernel,
        out_shape=jax.ShapeDtypeStruct((ROWS, D), BF16),
        in_specs=[far] * 5 + [near, near, scalar, near, near, near] + [far] * 5,
        out_specs=far,
        scratch_shapes=scratch,
        compiler_params=pltpu.CompilerParams(
            collective_id=0, has_side_effects=True, vmem_limit_bytes=60 * 1024 * 1024
        ),
        name="layer",
    )(
        residual,
        query_latent,
        query_rotary,
        cache_latent,
        cache_rotary,
        new_latent,
        new_rotary.T,
        cache_len,
        route_ids.T,
        routing_weight.T,
        norm_gain,
        value_up_matrix,
        out_weight,
        gate_weight,
        up_weight,
        down_weight,
    )


def solution(mesh):
    rows = P(("section", "expert"), None)
    placed = (
        rows,
        rows,
        rows,
        P(("section", "expert"), None, None),
        P(("section", "expert"), None, None),
        rows,
        P(None, ("section", "expert")),
        P(("section", "expert")),
        P("section", None),
        P("section", None),
        P("section", None),
        P("section", "expert", None, None),
        P("section", "expert", None),
        P("section", None, "expert"),
        P("section", None, "expert"),
        P("section", "expert", None),
    )
    return jax.shard_map(local, mesh=mesh, in_specs=placed, out_specs=rows, check_vma=False)
```

```python
import jax
import jax.numpy as jnp
from jax import lax
from jax.experimental import pallas as pl
from jax.experimental.pallas import tpu as pltpu
from jax.sharding import PartitionSpec as P

D = 3584
KVL = 512
ROPE = 64
VDIM = 128
HEADS = 128
TB = 4
SEQ = 4
ROWS = 16
CACHE = 512
FF_DEV = 256
SIDE = 4
GROUP = 32
BATCHES = 2
PARTS = 4
CHUNKS = BATCHES * PARTS
WIDTHS = (512, 384)
HALF = GROUP * ROWS // 2
SHORT = ROWS // BATCHES

BF16 = jnp.bfloat16
F32 = jnp.float32

FARTHEST_FIRST = sorted(
    [(i, j, k) for i in range(SIDE) for j in range(SIDE) for k in range(2) if i + j + k],
    key=lambda step: -min(step[0], SIDE - step[0]) - min(step[1], SIDE - step[1]),
)


def dot(a, b):
    return lax.dot_general(a, b, (((1,), (0,)), ((), ())), preferred_element_type=F32)


def dot_t(a, b):
    return lax.dot_general(a, b, (((1,), (1,)), ((), ())), preferred_element_type=F32)


def iota(shape, dim):
    return lax.broadcasted_iota(jnp.int32, shape, dim)


def kind(c):
    return c % PARTS // 2


def width(c):
    return WIDTHS[kind(c)]


class Chunked:
    def __init__(self, pair, place):
        self.pair, self.place = pair, place

    def find(self, index):
        index = index if isinstance(index, tuple) else (index,)
        c = index[self.place]
        slot = c // PARTS * 2 + c % 2
        return kind(c), index[: self.place] + (slot,) + index[self.place + 1 :]

    def __getitem__(self, index):
        which, index = self.find(index)
        return self.pair[which][index]

    def __setitem__(self, index, value):
        which, index = self.find(index)
        self.pair[which][index] = value

    @property
    def at(self):
        return Chunked([ref.at for ref in self.pair], self.place)


def layer_kernel(
    sections,
    residual_hbm,
    query_hbm,
    query_rot_hbm,
    latent_hbm,
    rotary_hbm,
    new_latent,
    new_rotary,
    cache_len,
    route_ids,
    routing_weight,
    norm_gain,
    value_up_hbm,
    out_weight_hbm,
    gate_hbm,
    up_hbm,
    down_hbm,
    out_hbm,
    residual,
    query,
    query_rot,
    latent,
    rotary,
    value_up,
    out_weight,
    gate_up,
    down,
    query_seq,
    rot_seq,
    keys_new,
    rot_new,
    context,
    arrived,
    diagonal,
    heads,
    chosen_all,
    chosen,
    cross_out_wide,
    cross_out_narrow,
    cross_in_wide,
    cross_in_narrow,
    first_out_wide,
    first_out_narrow,
    first_in_wide,
    first_in_narrow,
    second_out_wide,
    second_out_narrow,
    second_in_wide,
    second_in_narrow,
    hidden_wide,
    hidden_narrow,
    gathered_wide,
    gathered_narrow,
    hidden_units,
    activation,
    mixed_rows_wide,
    mixed_rows_narrow,
    handed_wide,
    handed_narrow,
    load_sem,
    context_send,
    context_recv,
    sum_send,
    sum_recv,
    gather_send,
    near_recv,
    far_recv,
    over_recv,
    hand_sem,
):
    cross_out = Chunked((cross_out_wide, cross_out_narrow), 1)
    cross_in = Chunked((cross_in_wide, cross_in_narrow), 1)
    first_out = Chunked((first_out_wide, first_out_narrow), 1)
    first_in = Chunked((first_in_wide, first_in_narrow), 1)
    second_out = Chunked((second_out_wide, second_out_narrow), 1)
    second_in = Chunked((second_in_wide, second_in_narrow), 1)
    hidden = Chunked((hidden_wide, hidden_narrow), 0)
    gathered = Chunked((gathered_wide, gathered_narrow), 0)
    mixed_rows = Chunked((mixed_rows_wide, mixed_rows_narrow), 0)
    handed = Chunked((handed_wide, handed_narrow), 0)
    section = lax.axis_index("section")
    me = lax.axis_index("expert")
    core = me % 2
    chip = me // 2
    x = chip // SIDE
    y = chip % SIDE
    sibling = chip * 2 + 1 - core

    def device(chip_x, chip_y):
        return (chip_x * SIDE + chip_y) * 2 + core

    barrier = pltpu.get_barrier_semaphore()

    @pl.loop(1, GROUP)
    def _(offset):
        pl.semaphore_signal(barrier, inc=1, device_id={"expert": (me + offset) % GROUP})

    if sections > 1:
        pl.semaphore_signal(barrier, inc=1, device_id={"section": (section + 1) % sections})
        pl.semaphore_signal(
            barrier, inc=1, device_id={"section": (section + sections - 1) % sections}
        )

    def load(source, target, sem):
        copy = pltpu.make_async_copy(source, target, sem)
        copy.start()
        return copy

    load_query = load(query_hbm, query, load_sem.at[0])
    load_rot = load(query_rot_hbm, query_rot, load_sem.at[1])
    load_latent = load(latent_hbm, latent, load_sem.at[2])
    load_rotary = load(rotary_hbm, rotary, load_sem.at[3])
    for j in range(4):
        load(value_up_hbm.at[0, j], value_up.at[:, pl.ds(j * VDIM, VDIM)], load_sem.at[4])
    load_out = load(out_weight_hbm.at[0], out_weight, load_sem.at[5])
    load_res = load(residual_hbm, residual, load_sem.at[6])
    load(gate_hbm.at[0], gate_up.at[:, pl.ds(0, FF_DEV)], load_sem.at[7])
    load(up_hbm.at[0], gate_up.at[:, pl.ds(FF_DEV, FF_DEV)], load_sem.at[7])
    load_down = load(down_hbm.at[0], down, load_sem.at[8])

    def settle(like, sem):
        pltpu.make_async_copy(like, like, sem).wait()

    keys_new[...] = jnp.zeros_like(keys_new)
    keys_new[pl.ds(0, ROWS), :] = new_latent[...]
    twice = (iota((ROPE, 128), 1) % ROPE == iota((ROPE, 128), 0)).astype(BF16)
    rot_new[...] = jnp.zeros_like(rot_new)
    rot_new[pl.ds(0, ROWS), :] = dot(new_rotary[...], twice).astype(BF16)

    expert = x
    weight_row = jnp.sum(
        jnp.where(route_ids[...] == expert, routing_weight[...], 0.0), axis=0, keepdims=True
    )
    chosen_all[...] = jnp.broadcast_to(weight_row, (128, GROUP * ROWS)).T
    for side in range(2):
        for place in range(GROUP // 2):
            source = (place * 2 + (core + side) % 2) * ROWS
            chosen[pl.ds((side * 16 + place) * ROWS, ROWS), :] = chosen_all[
                pl.ds(pl.multiple_of(source, ROWS), ROWS), :
            ]

    row_to = iota((256, 256), 0)
    row_from = iota((256, 256), 1)
    permute = (
        row_from == (row_to % 64) // TB * ROWS + row_to // 64 * TB + row_to % TB
    ).astype(BF16)
    low = iota((ROWS, 128), 1) < ROPE
    load_query.wait()
    load_rot.wait()
    for g in range(8):
        pieces, rot_pieces = [], []
        for h in range(g * 16, g * 16 + 16):
            pieces.append(query[:, pl.ds(h * KVL, KVL)])
            pair = query_rot[:, pl.ds(h // 2 * 128, 128)]
            keep = low if h % 2 == 0 else jnp.logical_not(low)
            rot_pieces.append(jnp.where(keep, pair, jnp.zeros_like(pair)))
        moved = dot(permute, jnp.concatenate(pieces, axis=0)).astype(BF16)
        moved_rot = dot(permute, jnp.concatenate(rot_pieces, axis=0)).astype(BF16)
        for b in range(SEQ):
            query_seq[b, pl.ds(g * 64, 64), :] = moved[b * 64 : b * 64 + 64]
            rot_seq[b, pl.ds(g * 64, 64), :] = moved_rot[b * 64 : b * 64 + 64]

    scale = (VDIM + ROPE) ** -0.5
    tile = 256

    def attend(b):
        keys = latent[b]
        rot_keys = jnp.concatenate([rotary[b], rotary[b]], axis=0)
        length = cache_len[b]
        for part in range(TB * HEADS // tile):
            rows = pl.ds(part * tile, tile)
            q = query_seq[b, rows, :]
            q_rot = rot_seq[b, rows, :]
            s = (dot_t(q, keys) + dot(q_rot, rot_keys)) * scale
            s_new = (dot_t(q, keys_new[...]) + dot_t(q_rot, rot_new[...])) * scale
            s = jnp.where(iota((tile, CACHE), 1) < length, s, -1e30)
            col = iota((tile, 128), 1)
            seen = jnp.logical_and(col // TB == b, col % TB <= iota((tile, 128), 0) % TB)
            s_new = jnp.where(seen, s_new, -1e30)
            top = jnp.maximum(
                jnp.max(s, axis=1, keepdims=True), jnp.max(s_new, axis=1, keepdims=True)
            )
            e = jnp.exp(s - top)
            e_new = jnp.exp(s_new - top)
            total = jnp.sum(e, axis=1, keepdims=True) + jnp.sum(e_new, axis=1, keepdims=True)
            mixed = dot(e.astype(BF16), keys) + dot(e_new.astype(BF16), keys_new[...])
            mixed = (mixed / total).astype(BF16)
            context[b, pl.ds(part * 2, 2)] = mixed.reshape(2, SIDE, 2, ROWS, KVL)

    def send(source, target, send_sem, recv_sem, to):
        pltpu.make_async_remote_copy(
            src_ref=source, dst_ref=target, send_sem=send_sem, recv_sem=recv_sem, device_id=to
        ).start()

    def scatter(b):
        arrived[b, 0, x, y] = context[b, x, y, core]

        for step_x, step_y, other in FARTHEST_FIRST:
            to_x, to_y, there = (x + step_x) % SIDE, (y + step_y) % SIDE, (core + other) % 2
            send(
                context.at[b, to_x, to_y, there],
                arrived.at[b, other, x, y],
                context_send.at[0],
                context_recv.at[b],
                {"expert": (to_x * SIDE + to_y) * 2 + there},
            )

    load_latent.wait()
    load_rotary.wait()
    attend(0)
    pl.semaphore_wait(barrier, GROUP - 1 + (2 if sections > 1 else 0))
    scatter(0)

    @pl.loop(1, SEQ)
    def _(b):
        attend(b)
        scatter(b)

    def columns(c, piece):
        start = piece * (D // 2) + c % 2 * (D // 4) + kind(c) * WIDTHS[0]
        return pl.ds(start, width(c))

    def stack(upper, lower):
        count = upper.shape[0] // SHORT
        pair = [part.reshape(count, SHORT, part.shape[1]) for part in (upper, lower)]
        return jnp.concatenate(pair, axis=1)

    def unstack(blocks):
        blocks = blocks.astype(F32)
        rows = blocks.shape[0] * SHORT
        return [
            blocks[:, SHORT * piece : SHORT * piece + SHORT].reshape(rows, blocks.shape[2])
            for piece in range(2)
        ]

    sent = pl.ds(0, (GROUP - 1) * ROWS)
    same_head = iota((512, 512), 0) % ROWS // TB == iota((512, 512), 1) // VDIM
    out_row = iota((64, 256), 0)
    in_row = iota((64, 256), 1)
    join = (
        (out_row // SHORT == in_row % 128 // ROWS)
        & (out_row % SHORT // TB == in_row // 128)
        & (out_row % TB == in_row % TB)
    ).astype(BF16)

    def raise_heads(batch):
        pair = range(2 * batch, 2 * batch + 2)
        for b in pair:
            settle(diagonal.at[b, sent], context_recv.at[b])
            product = dot(arrived[b].reshape(TB * HEADS, KVL), value_up[...])
            diagonal[b] = jnp.where(same_head, product, 0.0).astype(BF16)
        for g in range(4):
            group = jnp.concatenate([diagonal[b, pl.ds(g * 128, 128), :] for b in pair], axis=0)
            heads[batch, pl.ds(g * 64, 64), :] = dot(join, group).astype(BF16)

    def cross(which, c, partial):
        cross_out[which, c] = partial(c, 1).astype(BF16).reshape(HALF, width(c))
        send(
            cross_out.at[which, c],
            cross_in.at[which, c],
            sum_send.at[which, 0, kind(c)],
            sum_recv.at[which, c, 0],
            {"expert": sibling},
        )

    def along_first(which, c, partial):
        mine = partial(c, 0)
        settle(cross_in.at[which, c], sum_recv.at[which, c, 0])
        theirs = cross_in[which, c].reshape(GROUP // 2, ROWS, width(c)).astype(F32)
        first_out[which, c] = (mine + theirs).astype(BF16).reshape(SIDE, SIDE, ROWS, width(c))
        for half, step in ((0, 1), (1, SIDE - 1)):
            send(
                first_part(which, c, 2, half),
                first_in.at[which, c, 2, pl.ds(half * 2, 2)],
                sum_send.at[which, 1, kind(c)],
                sum_recv.at[which, c, 3],
                {"expert": ahead(c, step)},
            )
        for half, step in ((1, 1), (0, SIDE - 1)):
            to_neighbour(which, c, half, step)

    def line(c):
        return x if c % 2 == 0 else y

    def ahead(c, step):
        to = (line(c) + step) % SIDE
        return device(to, y) if c % 2 == 0 else device(x, to)

    def first_part(which, c, step, half):
        to = (line(c) + step) % SIDE
        pair = pl.ds(half * 2, 2)
        if c % 2 == 0:
            return first_out.at[which, c, to, pair]
        return first_out.at[which, c, pair, to]

    def to_neighbour(which, c, half, step):
        send(
            first_part(which, c, step, half),
            first_in.at[which, c, 0 if step == 1 else 1, pl.ds(half * 2, 2)],
            sum_send.at[which, 1, kind(c)],
            sum_recv.at[which, c, 1],
            {"expert": ahead(c, step)},
        )

    def relay_first(which, c):
        settle(first_in.at[which, c, 2], sum_recv.at[which, c, 3])
        for half, step in ((0, 1), (1, SIDE - 1)):
            part = first_part(which, c, step, half)
            through = first_in[which, c, 2, pl.ds(half * 2, 2)].astype(F32)
            part[...] = (part[...].astype(F32) + through).astype(BF16)
            to_neighbour(which, c, half, step)

    def along_second(which, c):
        settle(first_in.at[which, c, pl.ds(0, 2)], sum_recv.at[which, c, 1])
        if c % 2 == 0:
            rows = first_out[which, c, x].astype(F32)
        else:
            rows = first_out[which, c, :, y].astype(F32)
        for slot in range(2):
            rows = rows + first_in[which, c, slot].astype(F32)
        second_out[which, c] = rows.astype(BF16)
        for offset in range(1, SIDE):
            if c % 2 == 0:
                to = (y + offset) % SIDE
                where = device(x, to)
            else:
                to = (x + offset) % SIDE
                where = device(to, y)
            send(
                second_out.at[which, c, to],
                second_in.at[which, c, offset - 1],
                sum_send.at[which, 2, kind(c)],
                sum_recv.at[which, c, 2],
                {"expert": where},
            )

    def summed(which, c):
        settle(second_in.at[which, c], sum_recv.at[which, c, 2])
        rows = second_out[which, c, y if c % 2 == 0 else x].astype(F32)
        for slot in range(SIDE - 1):
            rows = rows + second_in[which, c, slot].astype(F32)
        return rows

    def chunks(batch):
        return range(batch * PARTS, batch * PARTS + PARTS)

    def projected(c, side):
        rows = heads[c // PARTS, pl.ds(side * HALF // 2, HALF // 2), :]
        return stack(*[dot(rows, out_weight[:, columns(c, piece)]) for piece in range(2)])

    def block(c, side, across):
        return gathered.at[c, side, across] if c % 2 == 0 else gathered.at[c, side, :, across]

    def normalise(batch):
        rows, squares = {}, 0.0
        half = slice(batch * SHORT, batch * SHORT + SHORT)
        for c in chunks(batch):
            left = [residual[:, columns(c, piece)].astype(F32)[half] for piece in range(2)]
            rows[c] = summed(0, c) + jnp.concatenate(left, axis=0)
            hidden[c] = rows[c]
            square = jnp.sum(rows[c] * rows[c], axis=1, keepdims=True)
            squares = squares + square[:SHORT] + square[SHORT:]
        factor = lax.rsqrt(squares * (1.0 / D) + 1e-06)
        factor = jnp.concatenate([factor, factor], axis=0)
        for c in chunks(batch):
            gain = jnp.concatenate(
                [
                    jnp.broadcast_to(norm_gain[:, columns(c, piece)], (SHORT, width(c)))
                    for piece in range(2)
                ],
                axis=0,
            )
            gathered[c, 0, x, y] = (rows[c] * factor * gain).astype(BF16)
            for offset in range(1, SIDE):
                to = (y if c % 2 == 0 else x) + offset
                send(
                    gathered.at[c, 0, x, y],
                    gathered.at[c, 0, x, y],
                    gather_send.at[0, kind(c)],
                    near_recv.at[c],
                    {"expert": device(x, to % SIDE) if c % 2 == 0 else device(to % SIDE, y)},
                )

    def to_sibling(c, across):
        send(
            block(c, 0, across),
            block(c, 1, across),
            gather_send.at[2, kind(c)],
            over_recv.at[c],
            {"expert": sibling},
        )

    def spread(c):
        settle(second_in.at[0, c], near_recv.at[c])
        here = line(c)
        for slot, step in ((1, 2), (0, 1), (2, 3)):
            send(
                block(c, 0, here),
                block(c, 0, here),
                gather_send.at[1, kind(c)],
                far_recv.at[c, slot],
                {"expert": ahead(c, step)},
            )
        to_sibling(c, here)

    def add_units(c, side):
        pieces = unstack(gathered[c, side].reshape(GROUP // 2, ROWS, width(c)))
        product = 0.0
        for piece in range(2):
            product = product + dot(pieces[piece].astype(BF16), gate_up[columns(c, piece), :])
        if c % PARTS == 0:
            hidden_units[c // PARTS, side] = product
        else:
            hidden_units[c // PARTS, side] = hidden_units[c // PARTS, side] + product

    def pass_on(c):
        here = line(c)
        for step in (1, 3, 2):
            settle(block(c, 0, here), far_recv.at[c, step - 1])
            to_sibling(c, (here + SIDE - step) % SIDE)
        add_units(c, 0)

    def take_over(c):
        settle(gathered.at[c, 1], over_recv.at[c])
        add_units(c, 1)

    def activate(batch, side):
        gate_value = hidden_units[batch, side, :, pl.ds(0, FF_DEV)]
        up_value = hidden_units[batch, side, :, pl.ds(FF_DEV, FF_DEV)]
        activation[batch, side] = (
            gate_value * jax.nn.sigmoid(gate_value) * up_value
        ).astype(BF16)

    def expert_share(c, side):
        batch = c // PARTS
        weight = chosen[pl.ds(side * HALF, HALF), :].reshape(GROUP // 2, ROWS, 128)
        weight = weight[:, batch * SHORT : batch * SHORT + SHORT].reshape(HALF // 2, 128)
        weight = jnp.concatenate([weight] * (width(c) // 128), axis=1)
        rows = activation[batch, side]
        return stack(*[dot(rows, down[:, columns(c, piece)]) * weight for piece in range(2)])

    def finish(c):
        rows = hidden[c] + summed(1, c)
        if c // PARTS == 0:
            mixed_rows[c] = rows
            return
        before = mixed_rows[c % PARTS]
        for piece in range(2):
            half = slice(piece * SHORT, piece * SHORT + SHORT)
            handed[c % PARTS, piece] = jnp.concatenate([before[half], rows[half]], axis=0).astype(BF16)
            target = out_hbm.at[:, columns(c, piece)]
            if sections > 1:
                send(
                    handed.at[c % PARTS, piece],
                    target,
                    hand_sem.at[0, kind(c)],
                    hand_sem.at[1, kind(c)],
                    {"section": (section + 1) % sections},
                )
            else:
                load(handed.at[c % PARTS, piece], target, hand_sem.at[0, kind(c)]).wait()

    settle(value_up, load_sem.at[4])

    def stage_heads(batch):
        raise_heads(batch)
        if batch == 0:
            load_out.wait()
        for c in chunks(batch):
            cross(0, c, projected)

    def stage_first(batch):
        for c in chunks(batch):
            along_first(0, c, projected)

    def stage_relay(batch):
        for c in chunks(batch):
            relay_first(0, c)

    def stage_second(batch):
        for c in chunks(batch):
            along_second(0, c)

    def stage_norm(batch):
        if batch == 0:
            load_res.wait()
        normalise(batch)

    def stage_spread(batch):
        for c in chunks(batch):
            spread(c)

    def stage_pass(batch):
        if batch == 0:
            settle(gate_up, load_sem.at[7])
        for c in chunks(batch):
            pass_on(c)

    def stage_units(batch):
        for c in chunks(batch):
            take_over(c)
        if batch == 0:
            load_down.wait()
        activate(batch, 1)
        for c in chunks(batch):
            cross(1, c, expert_share)

    def stage_shares(batch):
        activate(batch, 0)
        for c in chunks(batch):
            along_first(1, c, expert_share)

    def stage_through(batch):
        for c in chunks(batch):
            relay_first(1, c)

    def stage_last(batch):
        for c in chunks(batch):
            along_second(1, c)

    def stage_finish(batch):
        for c in chunks(batch):
            finish(c)

    stage_heads(0)
    stage_first(0)
    stage_heads(1)
    stage_relay(0)
    stage_first(1)
    stage_second(0)
    stage_relay(1)
    stage_norm(0)
    stage_second(1)
    stage_spread(0)
    stage_norm(1)
    stage_pass(0)
    stage_spread(1)
    stage_units(0)
    stage_shares(0)
    stage_pass(1)
    stage_units(1)
    stage_through(0)
    stage_shares(1)
    stage_last(0)
    stage_through(1)
    stage_last(1)
    stage_finish(0)
    stage_finish(1)

    settle(diagonal.at[:, sent], context_send.at[0])
    for size in range(2):
        for which in range(2):
            settle(cross_out.pair[size].at[which], sum_send.at[which, 0, size])
            settle(first_in.pair[size].at[which], sum_send.at[which, 1, size])
            settle(second_in.pair[size].at[which], sum_send.at[which, 2, size])
        settle(second_in.pair[size].at[0], gather_send.at[0, size])
        settle(first_in.pair[size].at[0], gather_send.at[1, size])
        settle(gathered.pair[size].at[:, 0], gather_send.at[2, size])
        if sections > 1:
            settle(handed.pair[size], hand_sem.at[0, size])
            settle(handed.pair[size], hand_sem.at[1, size])


def local(
    residual,
    query_latent,
    query_rotary,
    cache_latent,
    cache_rotary,
    new_latent,
    new_rotary,
    cache_len,
    route_ids,
    routing_weight,
    norm_gain,
    value_up_matrix,
    out_weight,
    gate_weight,
    up_weight,
    down_weight,
):
    sections = lax.axis_size("section")
    far = pl.BlockSpec(memory_space=pl.ANY)
    near = pl.BlockSpec(memory_space=pltpu.VMEM)
    scalar = pl.BlockSpec(memory_space=pltpu.SMEM)
    dma = pltpu.SemaphoreType.DMA
    scratch = [
        pltpu.VMEM((ROWS, D), BF16),
        pltpu.VMEM((ROWS, HEADS * KVL), BF16),
        pltpu.VMEM((ROWS, HEADS * ROPE), BF16),
        pltpu.VMEM((SEQ, CACHE, KVL), BF16),
        pltpu.VMEM((SEQ, ROPE, CACHE), BF16),
        pltpu.VMEM((KVL, 4 * VDIM), BF16),
        pltpu.VMEM((4 * VDIM, D), BF16),
        pltpu.VMEM((D, 2 * FF_DEV), BF16),
        pltpu.VMEM((FF_DEV, D), BF16),
        pltpu.VMEM((SEQ, TB * HEADS, KVL), BF16),
        pltpu.VMEM((SEQ, TB * HEADS, 128), BF16),
        pltpu.VMEM((128, KVL), BF16),
        pltpu.VMEM((128, 128), BF16),
        pltpu.VMEM((SEQ, SIDE, SIDE, 2, ROWS, KVL), BF16),
        pltpu.VMEM((SEQ, 2, SIDE, SIDE, ROWS, KVL), BF16),
        pltpu.VMEM((SEQ, TB * HEADS, KVL), BF16),
        pltpu.VMEM((BATCHES, HALF, 4 * VDIM), BF16),
        pltpu.VMEM((GROUP * ROWS, 128), F32),
        pltpu.VMEM((GROUP * ROWS, 128), F32),
        pltpu.VMEM((2, 2 * BATCHES, HALF, WIDTHS[0]), BF16),
        pltpu.VMEM((2, 2 * BATCHES, HALF, WIDTHS[1]), BF16),
        pltpu.VMEM((2, 2 * BATCHES, HALF, WIDTHS[0]), BF16),
        pltpu.VMEM((2, 2 * BATCHES, HALF, WIDTHS[1]), BF16),
        pltpu.VMEM((2, 2 * BATCHES, SIDE, SIDE, ROWS, WIDTHS[0]), BF16),
        pltpu.VMEM((2, 2 * BATCHES, SIDE, SIDE, ROWS, WIDTHS[1]), BF16),
        pltpu.VMEM((2, 2 * BATCHES, SIDE - 1, SIDE, ROWS, WIDTHS[0]), BF16),
        pltpu.VMEM((2, 2 * BATCHES, SIDE - 1, SIDE, ROWS, WIDTHS[1]), BF16),
        pltpu.VMEM((2, 2 * BATCHES, SIDE, ROWS, WIDTHS[0]), BF16),
        pltpu.VMEM((2, 2 * BATCHES, SIDE, ROWS, WIDTHS[1]), BF16),
        pltpu.VMEM((2, 2 * BATCHES, SIDE - 1, ROWS, WIDTHS[0]), BF16),
        pltpu.VMEM((2, 2 * BATCHES, SIDE - 1, ROWS, WIDTHS[1]), BF16),
        pltpu.VMEM((2 * BATCHES, ROWS, WIDTHS[0]), F32),
        pltpu.VMEM((2 * BATCHES, ROWS, WIDTHS[1]), F32),
        pltpu.VMEM((2 * BATCHES, 2, SIDE, SIDE, ROWS, WIDTHS[0]), BF16),
        pltpu.VMEM((2 * BATCHES, 2, SIDE, SIDE, ROWS, WIDTHS[1]), BF16),
        pltpu.VMEM((BATCHES, 2, HALF // 2, 2 * FF_DEV), F32),
        pltpu.VMEM((BATCHES, 2, HALF // 2, FF_DEV), BF16),
        pltpu.VMEM((2, ROWS, WIDTHS[0]), F32),
        pltpu.VMEM((2, ROWS, WIDTHS[1]), F32),
        pltpu.VMEM((2, 2, ROWS, WIDTHS[0]), BF16),
        pltpu.VMEM((2, 2, ROWS, WIDTHS[1]), BF16),
        dma((9,)),
        dma((1,)),
        dma((SEQ,)),
        dma((2, 3, 2)),
        dma((2, CHUNKS, 4)),
        dma((3, 2)),
        dma((CHUNKS,)),
        dma((CHUNKS, SIDE - 1)),
        dma((CHUNKS,)),
        dma((2, 2)),
    ]

    def kernel(*refs):
        layer_kernel(sections, *refs)

    return pl.pallas_call(
        kernel,
        out_shape=jax.ShapeDtypeStruct((ROWS, D), BF16),
        in_specs=[far] * 5 + [near, near, scalar, near, near, near] + [far] * 5,
        out_specs=far,
        scratch_shapes=scratch,
        compiler_params=pltpu.CompilerParams(
            collective_id=0, has_side_effects=True, vmem_limit_bytes=60 * 1024 * 1024
        ),
        name="layer",
    )(
        residual,
        query_latent,
        query_rotary,
        cache_latent,
        cache_rotary,
        new_latent,
        new_rotary.T,
        cache_len,
        route_ids.T,
        routing_weight.T,
        norm_gain,
        value_up_matrix,
        out_weight,
        gate_weight,
        up_weight,
        down_weight,
    )


def solution(mesh):
    rows = P(("section", "expert"), None)
    placed = (
        rows,
        rows,
        rows,
        P(("section", "expert"), None, None),
        P(("section", "expert"), None, None),
        rows,
        P(None, ("section", "expert")),
        P(("section", "expert")),
        P("section", None),
        P("section", None),
        P("section", None),
        P("section", "expert", None, None),
        P("section", "expert", None),
        P("section", None, "expert"),
        P("section", None, "expert"),
        P("section", "expert", None),
    )
    return jax.shard_map(local, mesh=mesh, in_specs=placed, out_specs=rows, check_vma=False)
```
